32 devices in a mesh: groups: 2 (over y), ctx: 4 (over z), head: 2 (over x), sub: 2 (over core).
Axes of the slice: x: 2, y: 2, z: 4, core: 2. Of those that a mesh axis runs over, the one named last changes fastest.
Arguments:
- hidden_in: bfloat16 [1024, 5120], P(('groups', 'ctx'), 'sub'), parts along dimension 0, may hold values from -6 to 6
- w_qkv: bfloat16 [5120, 8, 896], P('sub', 'head', 'ctx'), may hold values from -0.078125 to 0.078125
- qkv_bias: bfloat16 [8, 896], P('head'), may hold values from -3 to 3
- w_out: bfloat16 [8, 640, 5120], P('head', 'ctx'), may hold values from -0.078125 to 0.078125
- prev_keys: bfloat16 [1024, 8, 128], P(('groups', 'ctx', 'sub'), 'head'), parts along dimension 0, may hold values from -60 to 60
- prev_values: bfloat16 [1024, 8, 128], P(('groups', 'ctx', 'sub'), 'head'), parts along dimension 0, may hold values from -6 to 6
- shard_blocks: int32 [8], P('groups'), parts along dimension 0, may hold values from 0 to 3, each once
Outputs:
- attn_out: bfloat16 [1024, 5120], P(('groups', 'ctx', 'sub'), 'head'), parts along dimension 0
The draws below stay inside these ranges and needn't reach their ends.
There are 2 independent parts, one for each index of `groups`. The reference program is written for one: setup_inputs(seed, part) draws one part's arguments, and reference() takes and returns one part's arrays. A program takes and returns all parts, laid end to end along the dimension named above; an argument that names none is the same for every part. Nothing has to cross between parts.
Inputs may be any that keep to these rules, and one draw needn't show every extreme that they name: Index c of ctx holds the positions shard_blocks[c] * 128 to shard_blocks[c] * 128 + 127; every block occurs once.
All inputs are finite; a program needn't handle non-finite values.
Results may differ from the reference program's by a relative error of at most 0.015.
The reference program's roundings to bfloat16 on the way (of `head_out`) count: a program that leaves them out, or rounds other values in their place, can miss the bound.
Values may be sent and summed in bfloat16 or wider, within the bound.
A program may use at most 64 MiB of HBM per device.

```python
import jax
import jax.numpy as jnp
from jax import lax

D = 5120
KVH = 8
G = 5
HD = 128
TOK_CTX = 128
NPREV = 2
CH = 256
TOKENS = 512
N_CTX = 4
N_HEAD = 2


def draw_prev_keys(key, part):
    row_count = NPREV * CH
    drawn = jax.random.normal(key, (row_count, KVH, HD), jnp.float32)
    return jnp.clip(drawn, -60.0, 60.0).astype(jnp.bfloat16)


def steps_of(rng, dims, shards, smallest, high):
    level = 1.0
    for position, shards_of in shards:
        heights = jax.random.uniform(jax.random.fold_in(jax.random.fold_in(rng, 6), position), (shards_of,), jnp.float32, smallest / len(shards), high / len(shards))
        level = level * jnp.repeat(jnp.exp(heights), dims[position] // shards_of).reshape((-1,) + (1,) * (len(dims) - 1 - position))
    return level


def bell_draw(own_key, extent, scale, bound, shards=(), kind=jnp.bfloat16):
    array = scale * jax.random.normal(own_key, extent, jnp.float32)
    if shards:
        array = array * steps_of(own_key, extent, shards, -0.22, 0.18)
    return jnp.clip(array, -bound, bound).astype(kind)


def setup_inputs(seed: int = 0, part: int = 0) -> dict:
    splits = jax.random.split(jax.random.key(seed), 8)
    own_keys = jax.random.split(jax.random.fold_in(splits[7], part), 8)
    return {
        "hidden_in": bell_draw(own_keys[0], (TOKENS, D), 1.0, 6.0, ((0, 4), (1, 2))),
        "w_qkv": bell_draw(splits[1], (D, KVH, (G + 2) * HD), D ** -0.5, 0.078125, ((0, 2), (1, 2), (2, 4))),
        "qkv_bias": bell_draw(splits[2], (KVH, (G + 2) * HD), 0.5, 3.0, ((0, 2),)),
        "w_out": bell_draw(splits[3], (KVH, G * HD, D), (KVH * G * HD) ** -0.5, 0.078125, ((0, 2), (1, 4))),
        "prev_keys": draw_prev_keys(jax.random.fold_in(jax.random.fold_in(splits[7], part), 71), part),
        "prev_values": bell_draw(own_keys[5], (NPREV * CH, KVH, HD), 1.0, 6.0, ((0, 8), (1, 2))),
        "shard_blocks": jax.random.permutation(own_keys[6], N_CTX).astype(jnp.int32),
    }


rope_base = 10000000.0
neg_big = -1e30


def rotate(vectors, positions):
    half_width = vectors.shape[-1] // 2
    frequency = rope_base ** (-(jnp.arange(half_width, dtype=jnp.float32) * 2.0) / vectors.shape[-1])
    angles = positions.astype(jnp.float32)[:, None] * frequency[None, :]
    extra = (1,) * (vectors.ndim - 2)
    cosine = jnp.cos(angles).reshape((angles.shape[0],) + extra + (half_width,))
    sine_part = jnp.sin(angles).reshape((angles.shape[0],) + extra + (half_width,))
    first = vectors[..., :half_width]
    second = vectors[..., half_width:]
    return jnp.concatenate([first * cosine - second * sine_part, second * cosine + first * sine_part], axis=-1)


def attend(q_intra, q_succ, q_inter, span_row, local_row, cur_keys, cur_values, cur_span, cur_local, old_keys, old_values, old_span):
    row_count = q_intra.shape[0] * G
    score_scale = HD ** -0.5
    flat_intra = q_intra.reshape(row_count, HD)
    flat_succ = q_succ.reshape(row_count, HD)
    flat_inter = q_inter.reshape(row_count, HD)
    span_rep = jnp.repeat(span_row, G)
    local_rep = jnp.repeat(local_row, G)
    s_intra = jnp.dot(flat_intra, cur_keys.T, preferred_element_type=jnp.float32) * score_scale
    s_succ = jnp.dot(flat_succ, cur_keys.T, preferred_element_type=jnp.float32) * score_scale
    same_span = cur_span[None, :] == span_rep[:, None]
    before = cur_span[None, :] == span_rep[:, None] - 1
    allowed = (same_span & (cur_local[None, :] <= local_rep[:, None])) | before
    s_cur = jnp.where(same_span, s_intra, s_succ)
    o_succ = jnp.dot(flat_succ, old_keys.T, preferred_element_type=jnp.float32) * score_scale
    o_inter = jnp.dot(flat_inter, old_keys.T, preferred_element_type=jnp.float32) * score_scale
    s_old = jnp.where(old_span[None, :] == span_rep[:, None] - 1, o_succ, o_inter)
    running_max = jnp.maximum(jnp.max(jnp.where(allowed, s_cur, neg_big), axis=1), jnp.max(s_old, axis=1))
    w_cur = jnp.where(allowed, jnp.exp(s_cur - running_max[:, None]), 0.0)
    w_old = jnp.exp(s_old - running_max[:, None])
    weight_sum = jnp.sum(w_cur, axis=1) + jnp.sum(w_old, axis=1)
    weighted = jnp.dot(w_cur.astype(jnp.bfloat16), cur_values, preferred_element_type=jnp.float32)
    weighted = weighted + jnp.dot(w_old.astype(jnp.bfloat16), old_values, preferred_element_type=jnp.float32)
    head_out = (weighted / weight_sum[:, None]).astype(jnp.bfloat16)
    return head_out.reshape(q_intra.shape[0], G * HD)


def reference(hidden_in, w_qkv, qkv_bias, w_out, prev_keys, prev_values, shard_blocks):
    row_ids = jnp.arange(TOKENS, dtype=jnp.int32)
    owner = shard_blocks[row_ids // TOK_CTX]
    positions = owner * TOK_CTX + row_ids % TOK_CTX
    span_ids = NPREV + positions // CH
    local_pos = positions % CH
    joined = jnp.dot(hidden_in, w_qkv.reshape(D, KVH * (G + 2) * HD), preferred_element_type=jnp.float32)
    joined = joined.reshape(TOKENS, KVH, G + 2, HD) + qkv_bias.astype(jnp.float32).reshape(KVH, G + 2, HD)
    queries = joined[:, :, :G]
    q_intra = rotate(queries, local_pos).astype(jnp.bfloat16)
    q_succ = rotate(queries, local_pos + CH).astype(jnp.bfloat16)
    q_inter = rotate(queries, jnp.full((TOKENS,), 2 * CH - 1, jnp.int32)).astype(jnp.bfloat16)
    cur_keys = rotate(joined[:, :, G], local_pos).astype(jnp.bfloat16)
    cur_values = joined[:, :, G + 1].astype(jnp.bfloat16)
    old_rows = jnp.arange(NPREV * CH, dtype=jnp.int32)
    old_keys = rotate(prev_keys.astype(jnp.float32), old_rows % CH).astype(jnp.bfloat16)
    old_span = old_rows // CH

    def per_head(head_index):
        key_now = lax.dynamic_index_in_dim(cur_keys, head_index, 1, keepdims=False)
        value_now = lax.dynamic_index_in_dim(cur_values, head_index, 1, keepdims=False)
        key_old = lax.dynamic_index_in_dim(old_keys, head_index, 1, keepdims=False)
        value_old = lax.dynamic_index_in_dim(prev_values, head_index, 1, keepdims=False)
        intra_head = lax.dynamic_index_in_dim(q_intra, head_index, 1, keepdims=False)
        succ_head = lax.dynamic_index_in_dim(q_succ, head_index, 1, keepdims=False)
        inter_head = lax.dynamic_index_in_dim(q_inter, head_index, 1, keepdims=False)

        def per_block(block_index):
            first_row = (block_index * TOK_CTX).astype(jnp.int32)

            def take(values):
                return lax.dynamic_slice_in_dim(values, first_row, TOK_CTX, 0)

            return attend(take(intra_head), take(succ_head), take(inter_head), take(span_ids), take(local_pos),
                          key_now, value_now, span_ids, local_pos, key_old, value_old, old_span)

        return lax.map(per_block, jnp.arange(N_CTX, dtype=jnp.int32))

    attended = lax.map(per_head, jnp.arange(KVH, dtype=jnp.int32))
    attended = jnp.transpose(attended, (1, 2, 0, 3)).reshape(TOKENS, KVH * G * HD)
    group_rows = (KVH // N_HEAD) * G * HD
    w_flat = w_out.reshape(KVH * G * HD, D)
    result = jnp.zeros((TOKENS, D), jnp.float32)
    for group in range(N_HEAD):
        term = jnp.dot(attended[:, group * group_rows:(group + 1) * group_rows],
                       w_flat[group * group_rows:(group + 1) * group_rows], preferred_element_type=jnp.float32)
        result = result + lax.optimization_barrier(term.astype(jnp.bfloat16)).astype(jnp.float32)
    return result.astype(jnp.bfloat16)
```

```python
import functools
import math

import jax
import jax.numpy as jnp
import numpy as np
from jax import lax
from jax.experimental import pallas as pl
from jax.experimental.pallas import tpu as pltpu
from jax.sharding import PartitionSpec as P

G = 5
HD = 128
NPREV = 2


rope_base = 10000000.0
neg_big = -1e30


def rotate(vectors, positions):
    half_width = vectors.shape[-1] // 2
    frequency = rope_base ** (
        -(jnp.arange(half_width, dtype=jnp.float32) * 2.0) / vectors.shape[-1]
    )
    angles = positions.astype(jnp.float32)[:, None] * frequency[None, :]
    extra = (1,) * (vectors.ndim - 2)
    cosine = jnp.cos(angles).reshape((angles.shape[0],) + extra + (half_width,))
    sine_part = jnp.sin(angles).reshape((angles.shape[0],) + extra + (half_width,))
    first = vectors[..., :half_width]
    second = vectors[..., half_width:]
    return jnp.concatenate(
        [first * cosine - second * sine_part, second * cosine + first * sine_part], axis=-1
    )


def lookup(small_table, wanted):
    entries = jnp.arange(small_table.shape[0], dtype=jnp.int32)
    return jnp.sum(jnp.where(wanted[..., None] == entries, small_table, 0), axis=-1)


def local(hidden_in, w_qkv, qkv_bias, w_out, prev_keys, prev_values, shard_blocks):
    n_ctx = lax.axis_size("ctx")
    n_sub = lax.axis_size("sub")
    n_head = lax.axis_size("head")
    tok_ctx = hidden_in.shape[0]
    tok_dev = tok_ctx // n_sub
    span_len = tok_ctx * n_ctx // 2
    kv_dev = w_qkv.shape[1]
    me_ctx = lax.axis_index("ctx")
    me_sub = lax.axis_index("sub")
    partial_value = jnp.einsum(
        "td,dhn->thn",
        hidden_in,
        lax.all_gather(w_qkv, "ctx", axis=2, tiled=True),
        preferred_element_type=jnp.float32,
    )
    joined = lax.psum_scatter(partial_value, "sub", scatter_dimension=0, tiled=True)
    joined = (joined + qkv_bias.astype(jnp.float32)[None]).reshape(tok_dev, kv_dev, G + 2, HD)
    owner_block = lookup(shard_blocks, me_ctx)
    positions = owner_block * tok_ctx + me_sub * tok_dev + jnp.arange(tok_dev, dtype=jnp.int32)
    span_q = NPREV + positions // span_len
    local_q = positions % span_len
    queries = joined[:, :, :G]

    def arrange(rotated):
        return jnp.transpose(rotated.astype(jnp.bfloat16), (1, 0, 2, 3)).reshape(
            kv_dev, tok_dev * G, HD
        )

    q_intra = arrange(rotate(queries, local_q))
    q_succ = arrange(rotate(queries, local_q + span_len))
    q_inter = arrange(rotate(queries, jnp.full((tok_dev,), 2 * span_len - 1, jnp.int32)))
    k_cur = rotate(joined[:, :, G], local_q).astype(jnp.bfloat16)
    v_cur = joined[:, :, G + 1].astype(jnp.bfloat16)
    old_rows = (me_ctx * n_sub + me_sub) * tok_dev + jnp.arange(tok_dev, dtype=jnp.int32)
    k_prev = rotate(prev_keys.astype(jnp.float32), old_rows % span_len).astype(jnp.bfloat16)
    row_span = jnp.repeat(span_q, G)
    row_local = jnp.repeat(local_q, G)
    own_span = span_q[0]
    score_scale = HD ** (-0.5)
    row_count = tok_dev * G
    start_state = (
        jnp.full((kv_dev, row_count), neg_big, jnp.float32),
        jnp.zeros((kv_dev, row_count), jnp.float32),
        jnp.zeros((kv_dev, row_count, HD), jnp.float32),
    )

    def scores_of(query_set, key_block):
        return (
            jnp.einsum("hrd,khd->hrk", query_set, key_block, preferred_element_type=jnp.float32)
            * score_scale
        )

    def update(running, scores, allowed, value_block):
        running_max, weight_sum, weighted = running
        block_max = jnp.max(jnp.where(allowed, scores, neg_big), axis=2)
        new_max = jnp.maximum(running_max, block_max)
        weights = jnp.where(allowed, jnp.exp(scores - new_max[..., None]), 0.0)
        rescale = jnp.exp(running_max - new_max)
        weight_sum = weight_sum * rescale + jnp.sum(weights, axis=2)
        weighted = weighted * rescale[..., None] + jnp.einsum(
            "hrk,khd->hrd",
            weights.astype(jnp.bfloat16),
            value_block,
            preferred_element_type=jnp.float32,
        )
        return (new_max, weight_sum, weighted)

    def current_block(running, key_block, value_block, key_index):
        shard_index = key_index // tok_dev
        key_pos = (
            lookup(shard_blocks, shard_index // n_sub) * tok_ctx
            + shard_index % n_sub * tok_dev
            + key_index % tok_dev
        )
        key_span = NPREV + key_pos // span_len
        key_local = key_pos % span_len
        same_span = key_span[None, :] == row_span[:, None]
        before = key_span[None, :] == row_span[:, None] - 1
        allowed = same_span & (key_local[None, :] <= row_local[:, None]) | before
        query_set = jnp.where(key_span[0] == own_span, q_intra, q_succ)
        return update(running, scores_of(query_set, key_block), allowed[None], value_block)

    def earlier_block(running, key_block, value_block, key_index):
        block_span = key_index[0] // span_len
        query_set = jnp.where(block_span == own_span - 1, q_succ, q_inter)
        scores = scores_of(query_set, key_block)
        return update(running, scores, jnp.ones(scores.shape, jnp.bool_), value_block)

    cur_keys = lax.all_gather(k_cur, ("ctx", "sub"), axis=0, tiled=True)
    cur_values = lax.all_gather(v_cur, ("ctx", "sub"), axis=0, tiled=True)
    old_keys = lax.all_gather(k_prev, ("ctx", "sub"), axis=0, tiled=True)
    old_values = lax.all_gather(prev_values, ("ctx", "sub"), axis=0, tiled=True)
    piece_rows = cur_keys.shape[0]
    block_rows = math.gcd(piece_rows, tok_dev)

    def turn(turn_index, state_in):
        offset = turn_index * block_rows
        key_index = offset + jnp.arange(block_rows, dtype=jnp.int32)

        def take(values):
            return lax.dynamic_slice_in_dim(values, offset, block_rows, 0)

        state_in = current_block(state_in, take(cur_keys), take(cur_values), key_index)
        return earlier_block(state_in, take(old_keys), take(old_values), key_index)

    running_max, weight_sum, weighted = lax.fori_loop(
        0, piece_rows // block_rows, turn, start_state
    )
    head_out = (weighted / weight_sum[..., None]).astype(jnp.bfloat16)
    head_out = jnp.transpose(head_out.reshape(kv_dev, tok_dev, G, HD), (1, 0, 2, 3)).reshape(
        tok_dev, kv_dev, G * HD
    )
    group_cols = w_out.shape[2] // (n_head * n_sub)
    split_cols = w_out.reshape(kv_dev, w_out.shape[1], n_head, n_sub, group_cols)
    own_cols = lax.dynamic_index_in_dim(split_cols, me_sub, 3, keepdims=False).reshape(
        kv_dev, w_out.shape[1], n_head * group_cols
    )
    pair_heads = lax.all_gather(head_out, "sub", axis=0, tiled=True)
    summed = jnp.einsum(
        "thn,hnd->td",
        pair_heads,
        lax.all_gather(own_cols, "ctx", axis=1, tiled=True),
        preferred_element_type=jnp.float32,
    )
    shares = lax.psum_scatter(summed.astype(jnp.bfloat16), "head", scatter_dimension=1, tiled=True)
    return lax.all_to_all(shares, "sub", split_axis=0, concat_axis=1, tiled=True)


MESH = pl.DeviceIdType.MESH
LANE = 128
OUT_CHUNKS = 4


def round_up(value, step):
    return (value + step - 1) // step * step


def remote(src, dst, send_sem, recv_sem, **where):
    return pltpu.make_async_remote_copy(
        src_ref=src, dst_ref=dst, send_sem=send_sem, recv_sem=recv_sem,
        device_id=where, device_id_type=MESH,
    )


def rope_rows(vectors, cosine, sine):
    return vectors * cosine + pltpu.roll(vectors, HD // 2, 1) * sine


def fused(
    sb, x_ref, pv_ref, bias, rope_c, rope_s, w_hbm, wo_hbm, out_ref,
    hid, wv, wo, part, prcv, jb, ar, kv, old, qf, ho, a2, xs, xr, ow, zs, zr,
    w_sem, zsr_sem, zsl_sem, zrv_sem, hs_sem, hr_sem, ps_sem, pr_sem, as_sem, ar_sem,
    os_sem, or_sem, ex_sem, bs_sem, br_sem, cs_sem, cr_sem, ds_sem, dr_sem,
):
    n = hid.shape[0]
    tok = hid.shape[1]
    half = tok // 2
    span_len = tok * n // 2
    piece = w_hbm.shape[1]
    wide = wv.shape[1]
    rows_out = wo_hbm.shape[1]
    chunks, _, _, chunk = xs.shape
    c = lax.axis_index("ctx")
    hx = lax.axis_index("head")
    s = lax.axis_index("sub")
    oh = 1 - hx
    other = 1 - s

    def others(action):
        for j in range(n):
            pl.when(c != j)(functools.partial(action, j))

    for h in range(n):
        wv[h, piece:, :] = jnp.zeros((wide - piece, wv.shape[2]), jnp.bfloat16)
    load_w = pltpu.make_async_copy(w_hbm, wv.at[:, pl.ds(0, piece), :], w_sem.at[0])
    load_w.start()

    barrier = pltpu.get_barrier_semaphore()

    def greet(j):
        pl.semaphore_signal(barrier, inc=1, device_id={"ctx": j}, device_id_type=MESH)

    others(greet)
    pl.semaphore_signal(barrier, inc=1, device_id={"head": oh}, device_id_type=MESH)
    pl.semaphore_signal(barrier, inc=1, device_id={"sub": other}, device_id_type=MESH)
    pl.semaphore_wait(barrier, n + 1)

    mine = pl.ds(pl.multiple_of(hx * half, half), half)
    theirs = pl.ds(pl.multiple_of(oh * half, half), half)

    def to_right(src, blk):
        return remote(src, hid.at[blk, mine], zsr_sem.at[blk], zrv_sem.at[blk], ctx=c + 1)

    def to_left(src, blk):
        return remote(src, hid.at[blk, mine], zsl_sem.at[blk], zrv_sem.at[blk], ctx=c - 1)

    def over_x(blk, rows):
        return remote(hid.at[blk, rows], hid.at[blk, rows], hs_sem.at[blk], hr_sem.at[blk], head=oh)

    pl.when(c + 1 < n)(lambda: to_right(x_ref.at[mine], c).start())
    pl.when(c > 0)(lambda: to_left(x_ref.at[mine], c).start())

    def old_copy(j, src_ctx):
        return remote(pv_ref.at[j], old.at[s, src_ctx], os_sem.at[j], or_sem.at[src_ctx], ctx=j)

    others(lambda j: old_copy(j, c).start())
    old[s, c] = pv_ref[c]

    wo[...] = jnp.zeros(wo.shape, jnp.bfloat16)
    row_off = pl.multiple_of((c * rows_out) % LANE, 16)
    load_wo = pltpu.make_async_copy(wo_hbm, wo.at[:, pl.ds(row_off, rows_out), :], w_sem.at[1])
    load_wo.start()
    load_w.wait()

    def part_copy(blk):
        return remote(part.at[blk, other], prcv.at[blk], ps_sem.at[blk], pr_sem.at[blk], sub=other)

    def piece_copy(blk, j, src_ctx):
        return remote(
            jb.at[blk, j], ar.at[src_ctx, blk], as_sem.at[blk, j], ar_sem.at[src_ctx, blk], ctx=j
        )

    def project(blk, rows):
        for h in range(n):
            product = lax.dot_general(
                rows, wv[h], (((1,), (1,)), ((), ())), preferred_element_type=jnp.float32
            )
            part[blk, 0, h] = product[:half]
            part[blk, 1, h] = product[half:]
        part_copy(blk).start()

    def finish(blk):
        part_copy(blk).wait_recv()
        for h in range(n):
            joined = part[blk, s, h] + prcv[blk, h] + bias[h : h + 1, :]
            jb[blk, h] = joined.astype(jnp.bfloat16)
        ar[c, blk] = jb[blk, c]
        others(lambda j: piece_copy(blk, j, c).start())

    project(c, x_ref[...])
    finish(c)

    def arrive(distance, carry):
        left = c - distance
        right = c + distance

        def from_left():
            to_right(hid.at[left, mine], left).wait_recv()
            pl.when(c + 1 < n)(lambda: to_right(hid.at[left, mine], left).start())
            over_x(left, mine).start()

        def from_right():
            to_left(hid.at[right, mine], right).wait_recv()
            pl.when(c > 0)(lambda: to_left(hid.at[right, mine], right).start())
            over_x(right, mine).start()

        def use(blk):
            over_x(blk, theirs).wait_recv()
            project(blk, hid[blk])

        pl.when(left >= 0)(from_left)
        pl.when(right < n)(from_right)
        pl.when(left >= 0)(lambda: use(left))
        pl.when(right < n)(lambda: use(right))
        pl.when(left >= 0)(lambda: finish(left))
        pl.when(right < n)(lambda: finish(right))
        return carry

    lax.fori_loop(1, n, arrive, 0)

    def old_ready(j):
        old_copy(j, j).wait_recv()

    others(old_ready)
    for j in range(n):
        at = pl.ds(pl.multiple_of(((j * 2 + s) * half) % span_len, half), half)
        raw = old[s, j, 0].astype(jnp.float32)
        old[s, j, 0] = rope_rows(raw, rope_c[at, :], rope_s[at, :]).astype(jnp.bfloat16)
    old_pair = remote(old.at[s], old.at[s], ex_sem.at[0], ex_sem.at[1], sub=other)
    old_pair.start()

    lane = lax.broadcasted_iota(jnp.int32, (half, LANE), 1)

    def block_rows(table, in_span, first):
        chosen = None
        for v in range(n // 2):
            rows = table[pl.ds(pl.multiple_of(first + v * tok + s * half, half), half), :]
            chosen = rows if chosen is None else jnp.where(in_span == v, rows, chosen)
        return chosen

    def gather_head(blk, carry):
        others(lambda j: piece_copy(blk, j, j).wait_recv())
        got = [ar[j, blk].astype(jnp.float32) for j in range(n)]
        columns = []
        for b in range(G + 2):
            total = None
            for j in range(n):
                shift = b * LANE - j * piece
                if shift <= -LANE or shift >= piece:
                    continue
                moved = pltpu.roll(got[j], (-shift) % wide, 1)[:, :LANE]
                inside = (lane + shift >= 0) & (lane + shift < piece)
                moved = jnp.where(inside, moved, 0.0)
                total = moved if total is None else total + moved
            columns.append(total)
        for g in range(G):
            qf[blk, g] = columns[g]
        in_span = sb[blk] % (n // 2)
        cosine, sine = block_rows(rope_c, in_span, 0), block_rows(rope_s, in_span, 0)
        kv[s, 0, blk] = rope_rows(columns[G], cosine, sine).astype(jnp.bfloat16)
        kv[s, 1, blk] = columns[G + 1].astype(jnp.bfloat16)
        return carry

    lax.fori_loop(0, n, gather_head, 0)
    kv_pair = remote(kv.at[s], kv.at[s], ex_sem.at[2], ex_sem.at[3], sub=other)
    kv_pair.start()
    remote(old.at[other], old.at[other], ex_sem.at[0], ex_sem.at[1], sub=other).wait_recv()
    remote(kv.at[other], kv.at[other], ex_sem.at[2], ex_sem.at[3], sub=other).wait_recv()

    row_count = half * G
    scale = HD ** (-0.5)
    count = 2 * n * half
    key = lax.broadcasted_iota(jnp.int32, (1, count), 1)
    key_block = (key % (n * half)) // half
    key_pos = (key // (n * half)) * half + key % half
    for j in range(n):
        key_pos = key_pos + jnp.where(key_block == j, sb[j] * tok, 0)
    key_span = NPREV + key_pos // span_len
    key_local = key_pos % span_len
    row_in = lax.broadcasted_iota(jnp.int32, (row_count, 1), 0) % half
    last = 2 * span_len - 1

    def scores_of(query, keys):
        return lax.dot_general(
            query, keys, (((1,), (1,)), ((), ())), preferred_element_type=jnp.float32
        ) * scale

    def head_copy(blk, j, src_ctx):
        first = (j * rows_out) // LANE * LANE
        return remote(
            ho.at[blk, :, pl.ds(first, a2.shape[3])], a2.at[src_ctx, blk],
            bs_sem.at[blk, j], br_sem.at[src_ctx, blk], ctx=j,
        )

    def attend(blk, carry):
        first_pos = sb[blk] * tok
        span = NPREV + first_pos // span_len
        local_first = first_pos % span_len + s * half
        in_span = sb[blk] % (n // 2)

        def query_set(cosine, sine):
            return jnp.concatenate(
                [rope_rows(qf[blk, g], cosine, sine) for g in range(G)], axis=0
            ).astype(jnp.bfloat16)

        q_intra = query_set(block_rows(rope_c, in_span, 0), block_rows(rope_s, in_span, 0))
        q_succ = query_set(
            block_rows(rope_c, in_span, span_len), block_rows(rope_s, in_span, span_len)
        )
        q_inter = query_set(rope_c[last : last + 1, :], rope_s[last : last + 1, :])
        keys = kv[:, 0].reshape(2, n * half, HD).reshape(count, HD)
        values = kv[:, 1].reshape(2, n * half, HD).reshape(count, HD)
        same = key_span == span
        before = key_span == span - 1
        score = jnp.where(same, scores_of(q_intra, keys), scores_of(q_succ, keys))
        allowed = (same & (key_local <= row_in + local_first)) | before
        score = jnp.where(allowed, score, neg_big)
        pieces = [(score, values)]
        per_span = n // NPREV
        for b in range(NPREV):
            block = old[:, b * per_span : (b + 1) * per_span]
            size = 2 * per_span * half
            s_succ = scores_of(q_succ, block[:, :, 0].reshape(size, HD))
            s_inter = scores_of(q_inter, block[:, :, 0].reshape(size, HD))
            pieces.append((jnp.where(span - 1 == b, s_succ, s_inter), block[:, :, 1].reshape(size, HD)))
        top = functools.reduce(
            jnp.maximum, [jnp.max(score, axis=1, keepdims=True) for score, _ in pieces]
        )
        weight_sum = jnp.zeros((row_count, 1), jnp.float32)
        weighted = jnp.zeros((row_count, HD), jnp.float32)
        for score, value in pieces:
            weights = jnp.exp(score - top)
            weight_sum = weight_sum + jnp.sum(weights, axis=1, keepdims=True)
            weighted = weighted + jnp.dot(
                weights.astype(jnp.bfloat16), value, preferred_element_type=jnp.float32
            )
        result = (weighted / weight_sum).astype(jnp.bfloat16)
        for g in range(G):
            ho[blk, :, g * HD : (g + 1) * HD] = result[g * half : (g + 1) * half]

        def keep(j):
            first = (j * rows_out) // LANE * LANE
            a2[j, blk] = ho[blk, :, first : first + a2.shape[3]]

        for j in range(n):
            pl.when(c == j)(functools.partial(keep, j))
        others(lambda j: head_copy(blk, j, c).start())
        return carry

    lax.fori_loop(0, n, attend, 0)
    load_wo.wait()

    def heads_ready(blk, carry):
        others(lambda j: head_copy(blk, j, j).wait_recv())
        return carry

    lax.fori_loop(0, n, heads_ready, 0)

    def product(column_first):
        columns = pl.ds(pl.multiple_of(column_first, LANE), chunk)
        total = None
        for j in range(n):
            term = jnp.dot(
                a2[j].reshape(n * half, a2.shape[3]), wo[j, :, columns],
                preferred_element_type=jnp.float32,
            )
            total = term if total is None else total + term
        return total.reshape(n, half, chunk)

    width = chunk * chunks

    def x_copy(k):
        return remote(xs.at[k], xr.at[k], cs_sem.at[k], cr_sem.at[k], head=oh)

    def z_copy(k, j, src_ctx):
        return remote(
            zs.at[k, j], zr.at[src_ctx, k], ds_sem.at[k, j], dr_sem.at[src_ctx, k], ctx=j
        )

    def send_half(k, carry):
        xs[k] = product(oh * width + k * chunk).astype(jnp.bfloat16)
        x_copy(k).start()
        return carry

    def own_half(k, carry):
        ow[k] = product(hx * width + k * chunk)
        return carry

    def add_half(k, carry):
        x_copy(k).wait_recv()
        zs[k] = (ow[k] + xr[k].astype(jnp.float32)).astype(jnp.bfloat16)
        others(lambda j: z_copy(k, j, c).start())
        zr[c, k] = zs[k, c]
        return carry

    lax.fori_loop(0, chunks, send_half, 0)
    lax.fori_loop(0, chunks, own_half, 0)
    lax.fori_loop(0, chunks, add_half, 0)

    for k in range(chunks):
        others(lambda j: z_copy(k, j, j).wait_recv())
        total = zr[0, k].astype(jnp.float32)
        for j in range(1, n):
            total = total + zr[j, k].astype(jnp.float32)
        out_ref[:, k * chunk : (k + 1) * chunk] = total.astype(jnp.bfloat16)

    old_pair.wait_send()
    kv_pair.wait_send()
    others(lambda j: old_copy(j, c).wait_send())
    part_copy(c).wait_send()
    pl.when(c + 1 < n)(lambda: to_right(x_ref.at[mine], c).wait_send())
    pl.when(c > 0)(lambda: to_left(x_ref.at[mine], c).wait_send())

    def sent(distance, carry):
        left = c - distance
        right = c + distance

        def left_sent():
            pl.when(c + 1 < n)(lambda: to_right(hid.at[left, mine], left).wait_send())
            over_x(left, mine).wait_send()
            part_copy(left).wait_send()

        def right_sent():
            pl.when(c > 0)(lambda: to_left(hid.at[right, mine], right).wait_send())
            over_x(right, mine).wait_send()
            part_copy(right).wait_send()

        pl.when(left >= 0)(left_sent)
        pl.when(right < n)(right_sent)
        return carry

    lax.fori_loop(1, n, sent, 0)

    def block_sent(blk, carry):
        others(lambda j: piece_copy(blk, j, c).wait_send())
        others(lambda j: head_copy(blk, j, c).wait_send())
        return carry

    lax.fori_loop(0, n, block_sent, 0)

    def chunk_sent(k, carry):
        x_copy(k).wait_send()
        others(lambda j: z_copy(k, j, c).wait_send())
        return carry

    lax.fori_loop(0, chunks, chunk_sent, 0)


def rope_tables(count):
    frequency = np.float32(rope_base) ** (
        -(np.arange(HD // 2, dtype=np.float32) * np.float32(2.0)) / np.float32(HD)
    )
    angles = np.arange(count, dtype=np.float32)[:, None] * frequency.astype(np.float32)[None, :]
    cosine = np.cos(angles.astype(np.float64)).astype(np.float32)
    sine = np.sin(angles.astype(np.float64)).astype(np.float32)
    return (
        np.concatenate([cosine, cosine], axis=1),
        np.concatenate([-sine, sine], axis=1),
    )


def local_fused(hidden_in, w_qkv, qkv_bias, w_out, prev_keys, prev_values, shard_blocks):
    n = lax.axis_size("ctx")
    tok, features = hidden_in.shape
    half = tok // 2
    piece = w_qkv.shape[2]
    wide = round_up(piece, LANE)
    rows_out, model = w_out.shape[1:]
    window = 2 * LANE
    chunks = OUT_CHUNKS
    chunk = model // 2 // chunks
    c = lax.axis_index("ctx")
    bias = lax.dynamic_slice_in_dim(qkv_bias, c * piece, piece, 1).astype(jnp.float32)
    bias = jnp.pad(bias, ((0, 0), (0, wide - piece)))
    earlier = jnp.transpose(jnp.stack([prev_keys, prev_values]), (2, 0, 1, 3))
    cosine, sine = rope_tables(tok * n)
    bf16, f32, dma = jnp.bfloat16, jnp.float32, pltpu.SemaphoreType.DMA
    vmem = pl.BlockSpec(memory_space=pltpu.VMEM)
    smem = pl.BlockSpec(memory_space=pltpu.SMEM)
    hbm = pl.BlockSpec(memory_space=pl.ANY)
    return pl.pallas_call(
        fused,
        out_shape=jax.ShapeDtypeStruct((half, model // 2), bf16),
        in_specs=[smem, vmem, vmem, vmem, vmem, vmem, hbm, hbm],
        out_specs=vmem,
        scratch_shapes=[
            pltpu.VMEM((n, tok, features), bf16),
            pltpu.VMEM((n, wide, features), bf16),
            pltpu.VMEM((n, window, model), bf16),
            pltpu.VMEM((n, 2, n, half, wide), f32),
            pltpu.VMEM((n, n, half, wide), f32),
            pltpu.VMEM((n, n, half, wide), bf16),
            pltpu.VMEM((n, n, half, wide), bf16),
            pltpu.VMEM((2, 2, n, half, HD), bf16),
            pltpu.VMEM((2, n, 2, half, HD), bf16),
            pltpu.VMEM((n, G, half, HD), f32),
            pltpu.VMEM((n, half, G * HD), bf16),
            pltpu.VMEM((n, n, half, window), bf16),
            pltpu.VMEM((chunks, n, half, chunk), bf16),
            pltpu.VMEM((chunks, n, half, chunk), bf16),
            pltpu.VMEM((chunks, n, half, chunk), f32),
            pltpu.VMEM((chunks, n, half, chunk), bf16),
            pltpu.VMEM((n, chunks, half, chunk), bf16),
            dma((2,)), dma((n,)), dma((n,)), dma((n,)), dma((n,)), dma((n,)), dma((n,)), dma((n,)),
            dma((n, n)), dma((n, n)), dma((n,)), dma((n,)), dma((4,)), dma((n, n)), dma((n, n)),
            dma((chunks,)), dma((chunks,)), dma((chunks, n)), dma((n, chunks)),
        ],
        compiler_params=pltpu.CompilerParams(
            collective_id=0, has_side_effects=True, vmem_limit_bytes=56 * 2**20
        ),
    )(
        shard_blocks, hidden_in, earlier, bias, jnp.asarray(cosine), jnp.asarray(sine),
        jnp.transpose(w_qkv, (1, 2, 0)), w_out,
    )


def choose(hidden_in, w_qkv, qkv_bias, w_out, prev_keys, prev_values, shard_blocks):
    n = lax.axis_size("ctx")
    tok = hidden_in.shape[0]
    rows_out, model = w_out.shape[1:]
    offsets = [(j * rows_out) % LANE for j in range(n)]
    fits = (
        lax.axis_size("sub") == 2
        and lax.axis_size("head") == 2
        and w_qkv.shape[1] == n
        and n % NPREV == 0
        and tok % 32 == 0
        and w_qkv.shape[2] % 16 == 0
        and rows_out % 16 == 0
        and max(offsets) + rows_out <= 2 * LANE
        and ((n - 1) * rows_out) // LANE * LANE + 2 * LANE <= G * HD
        and model % (2 * OUT_CHUNKS * LANE) == 0
    )
    body = local_fused if fits else local
    return body(hidden_in, w_qkv, qkv_bias, w_out, prev_keys, prev_values, shard_blocks)


def solution(mesh):
    return jax.shard_map(
        choose,
        mesh=mesh,
        in_specs=(
            P(("groups", "ctx"), "sub"),
            P("sub", "head", "ctx"),
            P("head", None),
            P("head", "ctx", None),
            P(("groups", "ctx", "sub"), "head", None),
            P(("groups", "ctx", "sub"), "head", None),
            P("groups"),
        ),
        out_specs=P(("groups", "ctx", "sub"), "head"),
        check_vma=False,
    )
```

```python
import functools
import math

import jax
import jax.numpy as jnp
import numpy as np
from jax import lax
from jax.experimental import pallas as pl
from jax.experimental.pallas import tpu as pltpu
from jax.sharding import PartitionSpec as P

G = 5
HD = 128
NPREV = 2


rope_base = 10000000.0
neg_big = -1e30


def rotate(vectors, positions):
    half_width = vectors.shape[-1] // 2
    frequency = rope_base ** (
        -(jnp.arange(half_width, dtype=jnp.float32) * 2.0) / vectors.shape[-1]
    )
    angles = positions.astype(jnp.float32)[:, None] * frequency[None, :]
    extra = (1,) * (vectors.ndim - 2)
    cosine = jnp.cos(angles).reshape((angles.shape[0],) + extra + (half_width,))
    sine_part = jnp.sin(angles).reshape((angles.shape[0],) + extra + (half_width,))
    first = vectors[..., :half_width]
    second = vectors[..., half_width:]
    return jnp.concatenate(
        [first * cosine - second * sine_part, second * cosine + first * sine_part], axis=-1
    )


def lookup(small_table, wanted):
    entries = jnp.arange(small_table.shape[0], dtype=jnp.int32)
    return jnp.sum(jnp.where(wanted[..., None] == entries, small_table, 0), axis=-1)


def local(hidden_in, w_qkv, qkv_bias, w_out, prev_keys, prev_values, shard_blocks):
    n_ctx = lax.axis_size("ctx")
    n_sub = lax.axis_size("sub")
    n_head = lax.axis_size("head")
    tok_ctx = hidden_in.shape[0]
    tok_dev = tok_ctx // n_sub
    span_len = tok_ctx * n_ctx // 2
    kv_dev = w_qkv.shape[1]
    me_ctx = lax.axis_index("ctx")
    me_sub = lax.axis_index("sub")
    partial_value = jnp.einsum(
        "td,dhn->thn",
        hidden_in,
        lax.all_gather(w_qkv, "ctx", axis=2, tiled=True),
        preferred_element_type=jnp.float32,
    )
    joined = lax.psum_scatter(partial_value, "sub", scatter_dimension=0, tiled=True)
    joined = (joined + qkv_bias.astype(jnp.float32)[None]).reshape(tok_dev, kv_dev, G + 2, HD)
    owner_block = lookup(shard_blocks, me_ctx)
    positions = owner_block * tok_ctx + me_sub * tok_dev + jnp.arange(tok_dev, dtype=jnp.int32)
    span_q = NPREV + positions // span_len
    local_q = positions % span_len
    queries = joined[:, :, :G]

    def arrange(rotated):
        return jnp.transpose(rotated.astype(jnp.bfloat16), (1, 0, 2, 3)).reshape(
            kv_dev, tok_dev * G, HD
        )

    q_intra = arrange(rotate(queries, local_q))
    q_succ = arrange(rotate(queries, local_q + span_len))
    q_inter = arrange(rotate(queries, jnp.full((tok_dev,), 2 * span_len - 1, jnp.int32)))
    k_cur = rotate(joined[:, :, G], local_q).astype(jnp.bfloat16)
    v_cur = joined[:, :, G + 1].astype(jnp.bfloat16)
    old_rows = (me_ctx * n_sub + me_sub) * tok_dev + jnp.arange(tok_dev, dtype=jnp.int32)
    k_prev = rotate(prev_keys.astype(jnp.float32), old_rows % span_len).astype(jnp.bfloat16)
    row_span = jnp.repeat(span_q, G)
    row_local = jnp.repeat(local_q, G)
    own_span = span_q[0]
    score_scale = HD ** (-0.5)
    row_count = tok_dev * G
    start_state = (
        jnp.full((kv_dev, row_count), neg_big, jnp.float32),
        jnp.zeros((kv_dev, row_count), jnp.float32),
        jnp.zeros((kv_dev, row_count, HD), jnp.float32),
    )

    def scores_of(query_set, key_block):
        return (
            jnp.einsum("hrd,khd->hrk", query_set, key_block, preferred_element_type=jnp.float32)
            * score_scale
        )

    def update(running, scores, allowed, value_block):
        running_max, weight_sum, weighted = running
        block_max = jnp.max(jnp.where(allowed, scores, neg_big), axis=2)
        new_max = jnp.maximum(running_max, block_max)
        weights = jnp.where(allowed, jnp.exp(scores - new_max[..., None]), 0.0)
        rescale = jnp.exp(running_max - new_max)
        weight_sum = weight_sum * rescale + jnp.sum(weights, axis=2)
        weighted = weighted * rescale[..., None] + jnp.einsum(
            "hrk,khd->hrd",
            weights.astype(jnp.bfloat16),
            value_block,
            preferred_element_type=jnp.float32,
        )
        return (new_max, weight_sum, weighted)

    def current_block(running, key_block, value_block, key_index):
        shard_index = key_index // tok_dev
        key_pos = (
            lookup(shard_blocks, shard_index // n_sub) * tok_ctx
            + shard_index % n_sub * tok_dev
            + key_index % tok_dev
        )
        key_span = NPREV + key_pos // span_len
        key_local = key_pos % span_len
        same_span = key_span[None, :] == row_span[:, None]
        before = key_span[None, :] == row_span[:, None] - 1
        allowed = same_span & (key_local[None, :] <= row_local[:, None]) | before
        query_set = jnp.where(key_span[0] == own_span, q_intra, q_succ)
        return update(running, scores_of(query_set, key_block), allowed[None], value_block)

    def earlier_block(running, key_block, value_block, key_index):
        block_span = key_index[0] // span_len
        query_set = jnp.where(block_span == own_span - 1, q_succ, q_inter)
        scores = scores_of(query_set, key_block)
        return update(running, scores, jnp.ones(scores.shape, jnp.bool_), value_block)

    cur_keys = lax.all_gather(k_cur, ("ctx", "sub"), axis=0, tiled=True)
    cur_values = lax.all_gather(v_cur, ("ctx", "sub"), axis=0, tiled=True)
    old_keys = lax.all_gather(k_prev, ("ctx", "sub"), axis=0, tiled=True)
    old_values = lax.all_gather(prev_values, ("ctx", "sub"), axis=0, tiled=True)
    piece_rows = cur_keys.shape[0]
    block_rows = math.gcd(piece_rows, tok_dev)

    def turn(turn_index, state_in):
        offset = turn_index * block_rows
        key_index = offset + jnp.arange(block_rows, dtype=jnp.int32)

        def take(values):
            return lax.dynamic_slice_in_dim(values, offset, block_rows, 0)

        state_in = current_block(state_in, take(cur_keys), take(cur_values), key_index)
        return earlier_block(state_in, take(old_keys), take(old_values), key_index)

    running_max, weight_sum, weighted = lax.fori_loop(
        0, piece_rows // block_rows, turn, start_state
    )
    head_out = (weighted / weight_sum[..., None]).astype(jnp.bfloat16)
    head_out = jnp.transpose(head_out.reshape(kv_dev, tok_dev, G, HD), (1, 0, 2, 3)).reshape(
        tok_dev, kv_dev, G * HD
    )
    group_cols = w_out.shape[2] // (n_head * n_sub)
    split_cols = w_out.reshape(kv_dev, w_out.shape[1], n_head, n_sub, group_cols)
    own_cols = lax.dynamic_index_in_dim(split_cols, me_sub, 3, keepdims=False).reshape(
        kv_dev, w_out.shape[1], n_head * group_cols
    )
    pair_heads = lax.all_gather(head_out, "sub", axis=0, tiled=True)
    summed = jnp.einsum(
        "thn,hnd->td",
        pair_heads,
        lax.all_gather(own_cols, "ctx", axis=1, tiled=True),
        preferred_element_type=jnp.float32,
    )
    shares = lax.psum_scatter(summed.astype(jnp.bfloat16), "head", scatter_dimension=1, tiled=True)
    return lax.all_to_all(shares, "sub", split_axis=0, concat_axis=1, tiled=True)


MESH = pl.DeviceIdType.MESH
LANE = 128
OUT_CHUNKS = 5
ROW_PIECES = 2


def round_up(value, step):
    return (value + step - 1) // step * step


def remote(src, dst, send_sem, recv_sem, **where):
    return pltpu.make_async_remote_copy(
        src_ref=src, dst_ref=dst, send_sem=send_sem, recv_sem=recv_sem,
        device_id=where, device_id_type=MESH,
    )


def rope_rows(vectors, cosine, sine):
    return vectors * cosine + pltpu.roll(vectors, HD // 2, 1) * sine


def fused(
    sb, x_ref, pv_ref, bias, rope_c, rope_s, w_hbm, wo_hbm, out_ref,
    hid, wv, wo, part, prcv, jb, ar, kv, old, qf, ho, a2, xs, xr, ow, zs, zr,
    w_sem, zsr_sem, zsl_sem, zrv_sem, hs_sem, hr_sem, ps_sem, pr_sem, as_sem, ar_sem,
    os_sem, or_sem, ex_sem, bs_sem, br_sem, cs_sem, cr_sem, ds_sem, dr_sem,
):
    n = hid.shape[0]
    tok = hid.shape[1]
    half = tok // 2
    span_len = tok * n // 2
    piece = w_hbm.shape[1]
    wide = wv.shape[1]
    rows_out = wo_hbm.shape[1]
    chunks, _, _, chunk = xs.shape
    c = lax.axis_index("ctx")
    hx = lax.axis_index("head")
    s = lax.axis_index("sub")
    oh = 1 - hx
    other = 1 - s

    def others(action):
        for j in range(n):
            pl.when(c != j)(functools.partial(action, j))

    for h in range(n):
        wv[h, piece:, :] = jnp.zeros((wide - piece, wv.shape[2]), jnp.bfloat16)
    load_w = pltpu.make_async_copy(w_hbm, wv.at[:, pl.ds(0, piece), :], w_sem.at[0])
    load_w.start()

    barrier = pltpu.get_barrier_semaphore()

    def greet(j):
        pl.semaphore_signal(barrier, inc=1, device_id={"ctx": j}, device_id_type=MESH)

    others(greet)
    pl.semaphore_signal(barrier, inc=1, device_id={"head": oh}, device_id_type=MESH)
    pl.semaphore_signal(barrier, inc=1, device_id={"sub": other}, device_id_type=MESH)
    pl.semaphore_wait(barrier, n + 1)

    sliver = half // ROW_PIECES

    def rows_of(chip, p):
        return pl.ds(pl.multiple_of(chip * half + p * sliver, sliver), sliver)

    def to_right(src, blk, p):
        rows = rows_of(hx, p)
        return remote(
            src.at[rows], hid.at[blk, rows], zsr_sem.at[blk, p], zrv_sem.at[blk, p], ctx=c + 1
        )

    def to_left(src, blk, p):
        rows = rows_of(hx, p)
        return remote(
            src.at[rows], hid.at[blk, rows], zsl_sem.at[blk, p], zrv_sem.at[blk, p], ctx=c - 1
        )

    def over_x(blk, chip, p):
        rows = rows_of(chip, p)
        return remote(
            hid.at[blk, rows], hid.at[blk, rows], hs_sem.at[blk, p], hr_sem.at[blk, p], head=oh
        )

    for p in range(ROW_PIECES):
        pl.when(c + 1 < n)(lambda: to_right(x_ref, c, p).start())
        pl.when(c > 0)(lambda: to_left(x_ref, c, p).start())

    def old_copy(j, src_ctx):
        return remote(pv_ref.at[j], old.at[s, src_ctx], os_sem.at[j], or_sem.at[src_ctx], ctx=j)

    others(lambda j: old_copy(j, c).start())
    old[s, c] = pv_ref[c]

    wo[...] = jnp.zeros(wo.shape, jnp.bfloat16)
    row_off = pl.multiple_of((c * rows_out) % LANE, 16)
    load_wo = pltpu.make_async_copy(wo_hbm, wo.at[:, pl.ds(row_off, rows_out), :], w_sem.at[1])
    load_wo.start()
    load_w.wait()

    def part_copy(blk):
        return remote(part.at[blk, other], prcv.at[blk], ps_sem.at[blk], pr_sem.at[blk], sub=other)

    def piece_copy(blk, j, src_ctx):
        return remote(
            jb.at[blk, j], ar.at[src_ctx, blk], as_sem.at[blk, j], ar_sem.at[src_ctx, blk], ctx=j
        )

    def project(blk, rows):
        for h in range(n):
            product = lax.dot_general(
                rows, wv[h], (((1,), (1,)), ((), ())), preferred_element_type=jnp.float32
            )
            part[blk, 0, h] = product[:half]
            part[blk, 1, h] = product[half:]
        part_copy(blk).start()

    def finish(blk):
        part_copy(blk).wait_recv()
        for h in range(n):
            joined = part[blk, s, h] + prcv[blk, h] + bias[h : h + 1, :]
            jb[blk, h] = joined.astype(jnp.bfloat16)
        ar[c, blk] = jb[blk, c]
        others(lambda j: piece_copy(blk, j, c).start())

    def pass_on(distance, p):
        left = c - distance
        right = c + distance

        def from_left():
            to_right(hid.at[left], left, p).wait_recv()
            pl.when(c + 1 < n)(lambda: to_right(hid.at[left], left, p).start())
            over_x(left, hx, p).start()

        def from_right():
            to_left(hid.at[right], right, p).wait_recv()
            pl.when(c > 0)(lambda: to_left(hid.at[right], right, p).start())
            over_x(right, hx, p).start()

        pl.when(left >= 0)(from_left)
        pl.when(right < n)(from_right)

    def use(blk):
        for p in range(ROW_PIECES):
            over_x(blk, oh, p).wait_recv()
        project(blk, hid[blk])

    def both(distance, action, p=None):
        left = c - distance
        right = c + distance
        if p != 1:
            pl.when(left >= 0)(lambda: action(left))
        if p != 0:
            pl.when(right < n)(lambda: action(right))

    def arrive(distance, carry):
        pass_on(distance, 0)
        both(distance - 1, use, 0)
        pass_on(distance, 1)
        both(distance - 1, use, 1)
        pl.when(distance == 2)(lambda: finish(c))
        pl.when(distance > 2)(lambda: both(distance - 2, finish))
        return carry

    pass_on(1, 0)
    project(c, x_ref[...])
    pass_on(1, 1)
    lax.fori_loop(2, n, arrive, 0)
    both(n - 2, finish)
    both(n - 1, use)
    both(n - 1, finish)

    def old_ready(j):
        old_copy(j, j).wait_recv()

    others(old_ready)
    for j in range(n):
        at = pl.ds(pl.multiple_of(((j * 2 + s) * half) % span_len, half), half)
        raw = old[s, j, 0].astype(jnp.float32)
        old[s, j, 0] = rope_rows(raw, rope_c[at, :], rope_s[at, :]).astype(jnp.bfloat16)
    old_pair = remote(old.at[s], old.at[s], ex_sem.at[0], ex_sem.at[1], sub=other)
    old_pair.start()

    lane = lax.broadcasted_iota(jnp.int32, (half, LANE), 1)

    def block_rows(table, in_span, first):
        chosen = None
        for v in range(n // 2):
            rows = table[pl.ds(pl.multiple_of(first + v * tok + s * half, half), half), :]
            chosen = rows if chosen is None else jnp.where(in_span == v, rows, chosen)
        return chosen

    def gather_head(blk, carry):
        others(lambda j: piece_copy(blk, j, j).wait_recv())
        got = [ar[j, blk].astype(jnp.float32) for j in range(n)]
        columns = []
        for b in range(G + 2):
            total = None
            for j in range(n):
                shift = b * LANE - j * piece
                if shift <= -LANE or shift >= piece:
                    continue
                moved = pltpu.roll(got[j], (-shift) % wide, 1)[:, :LANE]
                inside = (lane + shift >= 0) & (lane + shift < piece)
                moved = jnp.where(inside, moved, 0.0)
                total = moved if total is None else total + moved
            columns.append(total)
        for g in range(G):
            qf[blk, g] = columns[g]
        in_span = sb[blk] % (n // 2)
        cosine, sine = block_rows(rope_c, in_span, 0), block_rows(rope_s, in_span, 0)
        kv[s, 0, blk] = rope_rows(columns[G], cosine, sine).astype(jnp.bfloat16)
        kv[s, 1, blk] = columns[G + 1].astype(jnp.bfloat16)
        return carry

    lax.fori_loop(0, n, gather_head, 0)
    kv_pair = remote(kv.at[s], kv.at[s], ex_sem.at[2], ex_sem.at[3], sub=other)
    kv_pair.start()
    remote(old.at[other], old.at[other], ex_sem.at[0], ex_sem.at[1], sub=other).wait_recv()
    remote(kv.at[other], kv.at[other], ex_sem.at[2], ex_sem.at[3], sub=other).wait_recv()

    row_count = half * G
    key = lax.broadcasted_iota(jnp.int32, (row_count, tok), 1)
    row = lax.broadcasted_iota(jnp.int32, (row_count, tok), 0) % half
    ahead = key - row
    last = 2 * span_len - 1
    power = HD ** (-0.5) * math.log2(math.e)

    def scores_of(query, keys):
        return lax.dot_general(
            query, keys, (((1,), (1,)), ((), ())), preferred_element_type=jnp.float32
        )

    def head_copy(blk, j, src_ctx):
        first = (j * rows_out) // LANE * LANE
        return remote(
            ho.at[blk, :, pl.ds(first, a2.shape[3])], a2.at[src_ctx, blk],
            bs_sem.at[blk, j], br_sem.at[src_ctx, blk], ctx=j,
        )

    def attend(blk, carry):
        first_pos = sb[blk] * tok
        span = NPREV + first_pos // span_len
        local_first = first_pos % span_len + s * half
        in_span = sb[blk] % (n // 2)

        def query_set(cosine, sine):
            return jnp.concatenate(
                [rope_rows(qf[blk, g], cosine, sine) for g in range(G)], axis=0
            ).astype(jnp.bfloat16)

        q_intra = query_set(block_rows(rope_c, in_span, 0), block_rows(rope_s, in_span, 0))
        q_succ = query_set(
            block_rows(rope_c, in_span, span_len), block_rows(rope_s, in_span, span_len)
        )
        q_inter = query_set(rope_c[last : last + 1, :], rope_s[last : last + 1, :])
        pieces = []
        for j in range(n):
            key_first = sb[j] * tok
            key_span = NPREV + key_first // span_len
            same = key_span == span
            reach = jnp.where(same, local_first - key_first % span_len, -2 * span_len)
            reach = jnp.where(key_span == span - 1, 2 * span_len, reach)
            query = jnp.where(same, q_intra, q_succ)
            score = scores_of(query, kv[:, 0, j].reshape(tok, HD))
            score = jnp.where(ahead <= reach, score, neg_big)
            pieces.append((score, kv[:, 1, j].reshape(tok, HD)))
        per_span = n // NPREV
        for b in range(NPREV):
            block = old[:, b * per_span : (b + 1) * per_span]
            size = 2 * per_span * half
            query = q_inter
            if b == NPREV - 1:
                query = jnp.where(span - 1 == b, q_succ, q_inter)
            score = scores_of(query, block[:, :, 0].reshape(size, HD))
            pieces.append((score, block[:, :, 1].reshape(size, HD)))
        top = functools.reduce(
            jnp.maximum, [jnp.max(score, axis=1, keepdims=True) for score, _ in pieces]
        )
        weight_sum = jnp.zeros((row_count, 1), jnp.float32)
        weighted = jnp.zeros((row_count, HD), jnp.float32)
        for score, value in pieces:
            weights = jnp.exp2((score - top) * power)
            weight_sum = weight_sum + jnp.sum(weights, axis=1, keepdims=True)
            weighted = weighted + jnp.dot(
                weights.astype(jnp.bfloat16), value, preferred_element_type=jnp.float32
            )
        result = (weighted / weight_sum).astype(jnp.bfloat16)
        for g in range(G):
            ho[blk, :, g * HD : (g + 1) * HD] = result[g * half : (g + 1) * half]

        def keep(j):
            first = (j * rows_out) // LANE * LANE
            a2[j, blk] = ho[blk, :, first : first + a2.shape[3]]

        for j in range(n):
            pl.when(c == j)(functools.partial(keep, j))
        others(lambda j: head_copy(blk, j, c).start())
        return carry

    lax.fori_loop(0, n, attend, 0)
    load_wo.wait()

    def heads_ready(blk, carry):
        others(lambda j: head_copy(blk, j, j).wait_recv())
        return carry

    lax.fori_loop(0, n, heads_ready, 0)

    def product(column_first):
        columns = pl.ds(pl.multiple_of(column_first, LANE), chunk)
        total = None
        for j in range(n):
            term = jnp.dot(
                a2[j].reshape(n * half, a2.shape[3]), wo[j, :, columns],
                preferred_element_type=jnp.float32,
            )
            total = term if total is None else total + term
        return total.reshape(n, half, chunk)

    width = chunk * chunks

    def x_copy(k):
        return remote(xs.at[k], xr.at[k], cs_sem.at[k], cr_sem.at[k], head=oh)

    def z_copy(k, j, src_ctx):
        return remote(
            zs.at[k, j], zr.at[src_ctx, k], ds_sem.at[k, j], dr_sem.at[src_ctx, k], ctx=j
        )

    def send_half(k, carry):
        xs[k] = product(oh * width + k * chunk).astype(jnp.bfloat16)
        x_copy(k).start()
        return carry

    def own_half(k, carry):
        ow[k] = product(hx * width + k * chunk)
        return carry

    def add_half(k, carry):
        x_copy(k).wait_recv()
        zs[k] = (ow[k] + xr[k].astype(jnp.float32)).astype(jnp.bfloat16)
        others(lambda j: z_copy(k, j, c).start())
        zr[c, k] = zs[k, c]
        return carry

    lax.fori_loop(0, chunks, send_half, 0)
    lax.fori_loop(0, chunks, own_half, 0)
    lax.fori_loop(0, chunks, add_half, 0)

    for k in range(chunks):
        others(lambda j: z_copy(k, j, j).wait_recv())
        total = zr[0, k].astype(jnp.float32)
        for j in range(1, n):
            total = total + zr[j, k].astype(jnp.float32)
        out_ref[:, k * chunk : (k + 1) * chunk] = total.astype(jnp.bfloat16)

    old_pair.wait_send()
    kv_pair.wait_send()
    others(lambda j: old_copy(j, c).wait_send())
    part_copy(c).wait_send()
    for p in range(ROW_PIECES):
        pl.when(c + 1 < n)(lambda: to_right(x_ref, c, p).wait_send())
        pl.when(c > 0)(lambda: to_left(x_ref, c, p).wait_send())

    def sent(distance, carry):
        left = c - distance
        right = c + distance

        def left_sent():
            for p in range(ROW_PIECES):
                pl.when(c + 1 < n)(lambda: to_right(hid.at[left], left, p).wait_send())
                over_x(left, hx, p).wait_send()
            part_copy(left).wait_send()

        def right_sent():
            for p in range(ROW_PIECES):
                pl.when(c > 0)(lambda: to_left(hid.at[right], right, p).wait_send())
                over_x(right, hx, p).wait_send()
            part_copy(right).wait_send()

        pl.when(left >= 0)(left_sent)
        pl.when(right < n)(right_sent)
        return carry

    lax.fori_loop(1, n, sent, 0)

    def block_sent(blk, carry):
        others(lambda j: piece_copy(blk, j, c).wait_send())
        others(lambda j: head_copy(blk, j, c).wait_send())
        return carry

    lax.fori_loop(0, n, block_sent, 0)

    def chunk_sent(k, carry):
        x_copy(k).wait_send()
        others(lambda j: z_copy(k, j, c).wait_send())
        return carry

    lax.fori_loop(0, chunks, chunk_sent, 0)


def rope_tables(count):
    frequency = np.float32(rope_base) ** (
        -(np.arange(HD // 2, dtype=np.float32) * np.float32(2.0)) / np.float32(HD)
    )
    angles = np.arange(count, dtype=np.float32)[:, None] * frequency.astype(np.float32)[None, :]
    cosine = np.cos(angles.astype(np.float64)).astype(np.float32)
    sine = np.sin(angles.astype(np.float64)).astype(np.float32)
    return (
        np.concatenate([cosine, cosine], axis=1),
        np.concatenate([-sine, sine], axis=1),
    )


def local_fused(hidden_in, w_qkv, qkv_bias, w_out, prev_keys, prev_values, shard_blocks):
    n = lax.axis_size("ctx")
    tok, features = hidden_in.shape
    half = tok // 2
    piece = w_qkv.shape[2]
    wide = round_up(piece, LANE)
    rows_out, model = w_out.shape[1:]
    window = 2 * LANE
    chunks = OUT_CHUNKS
    chunk = model // 2 // chunks
    c = lax.axis_index("ctx")
    bias = lax.dynamic_slice_in_dim(qkv_bias, c * piece, piece, 1).astype(jnp.float32)
    bias = jnp.pad(bias, ((0, 0), (0, wide - piece)))
    earlier = jnp.transpose(jnp.stack([prev_keys, prev_values]), (2, 0, 1, 3))
    cosine, sine = rope_tables(tok * n)
    bf16, f32, dma = jnp.bfloat16, jnp.float32, pltpu.SemaphoreType.DMA
    vmem = pl.BlockSpec(memory_space=pltpu.VMEM)
    smem = pl.BlockSpec(memory_space=pltpu.SMEM)
    hbm = pl.BlockSpec(memory_space=pl.ANY)
    return pl.pallas_call(
        fused,
        out_shape=jax.ShapeDtypeStruct((half, model // 2), bf16),
        in_specs=[smem, vmem, vmem, vmem, vmem, vmem, hbm, hbm],
        out_specs=vmem,
        scratch_shapes=[
            pltpu.VMEM((n, tok, features), bf16),
            pltpu.VMEM((n, wide, features), bf16),
            pltpu.VMEM((n, window, model), bf16),
            pltpu.VMEM((n, 2, n, half, wide), f32),
            pltpu.VMEM((n, n, half, wide), f32),
            pltpu.VMEM((n, n, half, wide), bf16),
            pltpu.VMEM((n, n, half, wide), bf16),
            pltpu.VMEM((2, 2, n, half, HD), bf16),
            pltpu.VMEM((2, n, 2, half, HD), bf16),
            pltpu.VMEM((n, G, half, HD), f32),
            pltpu.VMEM((n, half, G * HD), bf16),
            pltpu.VMEM((n, n, half, window), bf16),
            pltpu.VMEM((chunks, n, half, chunk), bf16),
            pltpu.VMEM((chunks, n, half, chunk), bf16),
            pltpu.VMEM((chunks, n, half, chunk), f32),
            pltpu.VMEM((chunks, n, half, chunk), bf16),
            pltpu.VMEM((n, chunks, half, chunk), bf16),
            dma((2,)), *[dma((n, ROW_PIECES))] * 5, dma((n,)), dma((n,)),
            dma((n, n)), dma((n, n)), dma((n,)), dma((n,)), dma((4,)), dma((n, n)), dma((n, n)),
            dma((chunks,)), dma((chunks,)), dma((chunks, n)), dma((n, chunks)),
        ],
        compiler_params=pltpu.CompilerParams(
            collective_id=0, has_side_effects=True, vmem_limit_bytes=56 * 2**20
        ),
    )(
        shard_blocks, hidden_in, earlier, bias, jnp.asarray(cosine), jnp.asarray(sine),
        jnp.transpose(w_qkv, (1, 2, 0)), w_out,
    )


def choose(hidden_in, w_qkv, qkv_bias, w_out, prev_keys, prev_values, shard_blocks):
    n = lax.axis_size("ctx")
    tok = hidden_in.shape[0]
    rows_out, model = w_out.shape[1:]
    offsets = [(j * rows_out) % LANE for j in range(n)]
    fits = (
        lax.axis_size("sub") == 2
        and lax.axis_size("head") == 2
        and w_qkv.shape[1] == n
        and n % NPREV == 0
        and n > 2
        and tok % (32 * ROW_PIECES) == 0
        and w_qkv.shape[2] % 16 == 0
        and rows_out % 16 == 0
        and max(offsets) + rows_out <= 2 * LANE
        and ((n - 1) * rows_out) // LANE * LANE + 2 * LANE <= G * HD
        and model % (2 * OUT_CHUNKS * LANE) == 0
    )
    body = local_fused if fits else local
    return body(hidden_in, w_qkv, qkv_bias, w_out, prev_keys, prev_values, shard_blocks)


def solution(mesh):
    return jax.shard_map(
        choose,
        mesh=mesh,
        in_specs=(
            P(("groups", "ctx"), "sub"),
            P("sub", "head", "ctx"),
            P("head", None),
            P("head", "ctx", None),
            P(("groups", "ctx", "sub"), "head", None),
            P(("groups", "ctx", "sub"), "head", None),
            P("groups"),
        ),
        out_specs=P(("groups", "ctx", "sub"), "head"),
        check_vma=False,
    )
```

```python
import functools
import math

import jax
import jax.numpy as jnp
import numpy as np
from jax import lax
from jax.experimental import pallas as pl
from jax.experimental.pallas import tpu as pltpu
from jax.sharding import PartitionSpec as P

G = 5
HD = 128
NPREV = 2


rope_base = 10000000.0
neg_big = -1e30


def rotate(vectors, positions):
    half_width = vectors.shape[-1] // 2
    frequency = rope_base ** (
        -(jnp.arange(half_width, dtype=jnp.float32) * 2.0) / vectors.shape[-1]
    )
    angles = positions.astype(jnp.float32)[:, None] * frequency[None, :]
    extra = (1,) * (vectors.ndim - 2)
    cosine = jnp.cos(angles).reshape((angles.shape[0],) + extra + (half_width,))
    sine_part = jnp.sin(angles).reshape((angles.shape[0],) + extra + (half_width,))
    first = vectors[..., :half_width]
    second = vectors[..., half_width:]
    return jnp.concatenate(
        [first * cosine - second * sine_part, second * cosine + first * sine_part], axis=-1
    )


def lookup(small_table, wanted):
    entries = jnp.arange(small_table.shape[0], dtype=jnp.int32)
    return jnp.sum(jnp.where(wanted[..., None] == entries, small_table, 0), axis=-1)


def local(hidden_in, w_qkv, qkv_bias, w_out, prev_keys, prev_values, shard_blocks):
    n_ctx = lax.axis_size("ctx")
    n_sub = lax.axis_size("sub")
    n_head = lax.axis_size("head")
    tok_ctx = hidden_in.shape[0]
    tok_dev = tok_ctx // n_sub
    span_len = tok_ctx * n_ctx // 2
    kv_dev = w_qkv.shape[1]
    me_ctx = lax.axis_index("ctx")
    me_sub = lax.axis_index("sub")
    partial_value = jnp.einsum(
        "td,dhn->thn",
        hidden_in,
        lax.all_gather(w_qkv, "ctx", axis=2, tiled=True),
        preferred_element_type=jnp.float32,
    )
    joined = lax.psum_scatter(partial_value, "sub", scatter_dimension=0, tiled=True)
    joined = (joined + qkv_bias.astype(jnp.float32)[None]).reshape(tok_dev, kv_dev, G + 2, HD)
    owner_block = lookup(shard_blocks, me_ctx)
    positions = owner_block * tok_ctx + me_sub * tok_dev + jnp.arange(tok_dev, dtype=jnp.int32)
    span_q = NPREV + positions // span_len
    local_q = positions % span_len
    queries = joined[:, :, :G]

    def arrange(rotated):
        return jnp.transpose(rotated.astype(jnp.bfloat16), (1, 0, 2, 3)).reshape(
            kv_dev, tok_dev * G, HD
        )

    q_intra = arrange(rotate(queries, local_q))
    q_succ = arrange(rotate(queries, local_q + span_len))
    q_inter = arrange(rotate(queries, jnp.full((tok_dev,), 2 * span_len - 1, jnp.int32)))
    k_cur = rotate(joined[:, :, G], local_q).astype(jnp.bfloat16)
    v_cur = joined[:, :, G + 1].astype(jnp.bfloat16)
    old_rows = (me_ctx * n_sub + me_sub) * tok_dev + jnp.arange(tok_dev, dtype=jnp.int32)
    k_prev = rotate(prev_keys.astype(jnp.float32), old_rows % span_len).astype(jnp.bfloat16)
    row_span = jnp.repeat(span_q, G)
    row_local = jnp.repeat(local_q, G)
    own_span = span_q[0]
    score_scale = HD ** (-0.5)
    row_count = tok_dev * G
    start_state = (
        jnp.full((kv_dev, row_count), neg_big, jnp.float32),
        jnp.zeros((kv_dev, row_count), jnp.float32),
        jnp.zeros((kv_dev, row_count, HD), jnp.float32),
    )

    def scores_of(query_set, key_block):
        return (
            jnp.einsum("hrd,khd->hrk", query_set, key_block, preferred_element_type=jnp.float32)
            * score_scale
        )

    def update(running, scores, allowed, value_block):
        running_max, weight_sum, weighted = running
        block_max = jnp.max(jnp.where(allowed, scores, neg_big), axis=2)
        new_max = jnp.maximum(running_max, block_max)
        weights = jnp.where(allowed, jnp.exp(scores - new_max[..., None]), 0.0)
        rescale = jnp.exp(running_max - new_max)
        weight_sum = weight_sum * rescale + jnp.sum(weights, axis=2)
        weighted = weighted * rescale[..., None] + jnp.einsum(
            "hrk,khd->hrd",
            weights.astype(jnp.bfloat16),
            value_block,
            preferred_element_type=jnp.float32,
        )
        return (new_max, weight_sum, weighted)

    def current_block(running, key_block, value_block, key_index):
        shard_index = key_index // tok_dev
        key_pos = (
            lookup(shard_blocks, shard_index // n_sub) * tok_ctx
            + shard_index % n_sub * tok_dev
            + key_index % tok_dev
        )
        key_span = NPREV + key_pos // span_len
        key_local = key_pos % span_len
        same_span = key_span[None, :] == row_span[:, None]
        before = key_span[None, :] == row_span[:, None] - 1
        allowed = same_span & (key_local[None, :] <= row_local[:, None]) | before
        query_set = jnp.where(key_span[0] == own_span, q_intra, q_succ)
        return update(running, scores_of(query_set, key_block), allowed[None], value_block)

    def earlier_block(running, key_block, value_block, key_index):
        block_span = key_index[0] // span_len
        query_set = jnp.where(block_span == own_span - 1, q_succ, q_inter)
        scores = scores_of(query_set, key_block)
        return update(running, scores, jnp.ones(scores.shape, jnp.bool_), value_block)

    cur_keys = lax.all_gather(k_cur, ("ctx", "sub"), axis=0, tiled=True)
    cur_values = lax.all_gather(v_cur, ("ctx", "sub"), axis=0, tiled=True)
    old_keys = lax.all_gather(k_prev, ("ctx", "sub"), axis=0, tiled=True)
    old_values = lax.all_gather(prev_values, ("ctx", "sub"), axis=0, tiled=True)
    piece_rows = cur_keys.shape[0]
    block_rows = math.gcd(piece_rows, tok_dev)

    def turn(turn_index, state_in):
        offset = turn_index * block_rows
        key_index = offset + jnp.arange(block_rows, dtype=jnp.int32)

        def take(values):
            return lax.dynamic_slice_in_dim(values, offset, block_rows, 0)

        state_in = current_block(state_in, take(cur_keys), take(cur_values), key_index)
        return earlier_block(state_in, take(old_keys), take(old_values), key_index)

    running_max, weight_sum, weighted = lax.fori_loop(
        0, piece_rows // block_rows, turn, start_state
    )
    head_out = (weighted / weight_sum[..., None]).astype(jnp.bfloat16)
    head_out = jnp.transpose(head_out.reshape(kv_dev, tok_dev, G, HD), (1, 0, 2, 3)).reshape(
        tok_dev, kv_dev, G * HD
    )
    group_cols = w_out.shape[2] // (n_head * n_sub)
    split_cols = w_out.reshape(kv_dev, w_out.shape[1], n_head, n_sub, group_cols)
    own_cols = lax.dynamic_index_in_dim(split_cols, me_sub, 3, keepdims=False).reshape(
        kv_dev, w_out.shape[1], n_head * group_cols
    )
    pair_heads = lax.all_gather(head_out, "sub", axis=0, tiled=True)
    summed = jnp.einsum(
        "thn,hnd->td",
        pair_heads,
        lax.all_gather(own_cols, "ctx", axis=1, tiled=True),
        preferred_element_type=jnp.float32,
    )
    shares = lax.psum_scatter(summed.astype(jnp.bfloat16), "head", scatter_dimension=1, tiled=True)
    return lax.all_to_all(shares, "sub", split_axis=0, concat_axis=1, tiled=True)


MESH = pl.DeviceIdType.MESH
LANE = 128
OUT_CHUNKS = 5
ROW_PIECES = 2


def round_up(value, step):
    return (value + step - 1) // step * step


def remote(src, dst, send_sem, recv_sem, **where):
    return pltpu.make_async_remote_copy(
        src_ref=src, dst_ref=dst, send_sem=send_sem, recv_sem=recv_sem,
        device_id=where, device_id_type=MESH,
    )


def rope_rows(vectors, cosine, sine):
    return vectors * cosine + pltpu.roll(vectors, HD // 2, 1) * sine


def fused(
    sb, x_ref, pv_ref, bias, rope_c, rope_s, w_hbm, wo_hbm, out_ref,
    hid, wv, wo, part, prcv, jb, ar, kv, old, qf, ho, a2, xs, xr, ow, zs, zr,
    w_sem, zsr_sem, zsl_sem, zrv_sem, hs_sem, hr_sem, ps_sem, pr_sem, as_sem, ar_sem,
    os_sem, or_sem, ex_sem, bs_sem, br_sem, cs_sem, cr_sem, ds_sem, dr_sem,
):
    n = hid.shape[0]
    tok = hid.shape[1]
    half = tok // 2
    span_len = tok * n // 2
    piece = w_hbm.shape[1]
    wide = wv.shape[1]
    rows_out = wo_hbm.shape[1]
    per_half = xs.shape[1]
    chunk = xs.shape[3]
    chunks = zr.shape[1]
    c = lax.axis_index("ctx")
    hx = lax.axis_index("head")
    s = lax.axis_index("sub")
    oh = 1 - hx
    other = 1 - s

    def others(action):
        for j in range(n):
            pl.when(c != j)(functools.partial(action, j))

    for h in range(n):
        wv[h, piece:, :] = jnp.zeros((wide - piece, wv.shape[2]), jnp.bfloat16)
    load_w = pltpu.make_async_copy(w_hbm, wv.at[:, pl.ds(0, piece), :], w_sem.at[0])
    load_w.start()

    barrier = pltpu.get_barrier_semaphore()

    def greet(j):
        pl.semaphore_signal(barrier, inc=1, device_id={"ctx": j}, device_id_type=MESH)

    others(greet)
    pl.semaphore_signal(barrier, inc=1, device_id={"head": oh}, device_id_type=MESH)
    pl.semaphore_signal(barrier, inc=1, device_id={"sub": other}, device_id_type=MESH)
    pl.semaphore_wait(barrier, n + 1)

    sliver = half // ROW_PIECES

    def rows_of(chip, p):
        return pl.ds(pl.multiple_of(chip * half + p * sliver, sliver), sliver)

    def to_right(src, blk, p):
        rows = rows_of(hx, p)
        return remote(
            src.at[rows], hid.at[blk, rows], zsr_sem.at[blk, p], zrv_sem.at[blk, p], ctx=c + 1
        )

    def to_left(src, blk, p):
        rows = rows_of(hx, p)
        return remote(
            src.at[rows], hid.at[blk, rows], zsl_sem.at[blk, p], zrv_sem.at[blk, p], ctx=c - 1
        )

    def over_x(blk, chip, p):
        rows = rows_of(chip, p)
        return remote(
            hid.at[blk, rows], hid.at[blk, rows], hs_sem.at[blk, p], hr_sem.at[blk, p], head=oh
        )

    for p in range(ROW_PIECES):
        pl.when(c + 1 < n)(lambda: to_right(x_ref, c, p).start())
        pl.when(c > 0)(lambda: to_left(x_ref, c, p).start())

    def old_copy(j, src_ctx):
        return remote(pv_ref.at[j], old.at[s, src_ctx], os_sem.at[j], or_sem.at[src_ctx], ctx=j)

    others(lambda j: old_copy(j, c).start())
    old[s, c] = pv_ref[c]

    wo[...] = jnp.zeros(wo.shape, jnp.bfloat16)
    row_off = pl.multiple_of((c * rows_out) % LANE, 16)
    load_wo = pltpu.make_async_copy(wo_hbm, wo.at[:, pl.ds(row_off, rows_out), :], w_sem.at[1])
    load_wo.start()
    load_w.wait()

    def part_copy(blk):
        return remote(part.at[blk, other], prcv.at[blk], ps_sem.at[blk], pr_sem.at[blk], sub=other)

    def piece_copy(blk, j, src_ctx):
        return remote(
            jb.at[blk, j], ar.at[src_ctx, blk], as_sem.at[blk, j], ar_sem.at[src_ctx, blk], ctx=j
        )

    def project(blk, rows):
        for h in range(n):
            product = lax.dot_general(
                rows, wv[h], (((1,), (1,)), ((), ())), preferred_element_type=jnp.float32
            )
            part[blk, 0, h] = product[:half]
            part[blk, 1, h] = product[half:]
        part_copy(blk).start()

    def finish(blk):
        part_copy(blk).wait_recv()
        for h in range(n):
            joined = part[blk, s, h] + prcv[blk, h] + bias[h : h + 1, :]
            jb[blk, h] = joined.astype(jnp.bfloat16)
        ar[c, blk] = jb[blk, c]
        others(lambda j: piece_copy(blk, j, c).start())

    def pass_on(distance, p):
        left = c - distance
        right = c + distance

        def from_left():
            to_right(hid.at[left], left, p).wait_recv()
            pl.when(c + 1 < n)(lambda: to_right(hid.at[left], left, p).start())
            over_x(left, hx, p).start()

        def from_right():
            to_left(hid.at[right], right, p).wait_recv()
            pl.when(c > 0)(lambda: to_left(hid.at[right], right, p).start())
            over_x(right, hx, p).start()

        pl.when(left >= 0)(from_left)
        pl.when(right < n)(from_right)

    def use(blk):
        for p in range(ROW_PIECES):
            over_x(blk, oh, p).wait_recv()
        project(blk, hid[blk])

    def both(distance, action, p=None):
        left = c - distance
        right = c + distance
        if p != 1:
            pl.when(left >= 0)(lambda: action(left))
        if p != 0:
            pl.when(right < n)(lambda: action(right))

    def arrive(distance, carry):
        pass_on(distance, 0)
        both(distance - 1, use, 0)
        pass_on(distance, 1)
        both(distance - 1, use, 1)
        pl.when(distance == 2)(lambda: finish(c))
        pl.when(distance > 2)(lambda: both(distance - 2, finish))
        return carry

    pass_on(1, 0)
    project(c, x_ref[...])
    pass_on(1, 1)
    lax.fori_loop(2, n, arrive, 0)
    both(n - 2, finish)
    both(n - 1, use)
    both(n - 1, finish)

    def old_ready(j):
        old_copy(j, j).wait_recv()

    others(old_ready)
    for j in range(n):
        at = pl.ds(pl.multiple_of(((j * 2 + s) * half) % span_len, half), half)
        raw = old[s, j, 0].astype(jnp.float32)
        old[s, j, 0] = rope_rows(raw, rope_c[at, :], rope_s[at, :]).astype(jnp.bfloat16)
    old_pair = remote(old.at[s], old.at[s], ex_sem.at[0], ex_sem.at[1], sub=other)
    old_pair.start()

    lane = lax.broadcasted_iota(jnp.int32, (half, LANE), 1)

    def block_rows(table, in_span, first):
        chosen = None
        for v in range(n // 2):
            rows = table[pl.ds(pl.multiple_of(first + v * tok + s * half, half), half), :]
            chosen = rows if chosen is None else jnp.where(in_span == v, rows, chosen)
        return chosen

    def gather_head(blk, carry):
        others(lambda j: piece_copy(blk, j, j).wait_recv())
        got = [ar[j, blk].astype(jnp.float32) for j in range(n)]
        columns = []
        for b in range(G + 2):
            total = None
            for j in range(n):
                shift = b * LANE - j * piece
                if shift <= -LANE or shift >= piece:
                    continue
                moved = pltpu.roll(got[j], (-shift) % wide, 1)[:, :LANE]
                inside = (lane + shift >= 0) & (lane + shift < piece)
                moved = jnp.where(inside, moved, 0.0)
                total = moved if total is None else total + moved
            columns.append(total)
        for g in range(G):
            qf[blk, g] = columns[g]
        in_span = sb[blk] % (n // 2)
        cosine, sine = block_rows(rope_c, in_span, 0), block_rows(rope_s, in_span, 0)
        kv[s, 0, blk] = rope_rows(columns[G], cosine, sine).astype(jnp.bfloat16)
        kv[s, 1, blk] = columns[G + 1].astype(jnp.bfloat16)
        return carry

    lax.fori_loop(0, n, gather_head, 0)
    kv_pair = remote(kv.at[s], kv.at[s], ex_sem.at[2], ex_sem.at[3], sub=other)
    kv_pair.start()
    remote(old.at[other], old.at[other], ex_sem.at[0], ex_sem.at[1], sub=other).wait_recv()
    remote(kv.at[other], kv.at[other], ex_sem.at[2], ex_sem.at[3], sub=other).wait_recv()

    row_count = half * G
    key = lax.broadcasted_iota(jnp.int32, (row_count, tok), 1)
    row = lax.broadcasted_iota(jnp.int32, (row_count, tok), 0) % half
    ahead = key - row
    last = 2 * span_len - 1
    power = HD ** (-0.5) * math.log2(math.e)

    def scores_of(query, keys):
        return lax.dot_general(
            query, keys, (((1,), (1,)), ((), ())), preferred_element_type=jnp.float32
        )

    def head_copy(blk, j, src_ctx):
        first = (j * rows_out) // LANE * LANE
        return remote(
            ho.at[blk, :, pl.ds(first, a2.shape[3])], a2.at[src_ctx, blk],
            bs_sem.at[blk, j], br_sem.at[src_ctx, blk], ctx=j,
        )

    def attend(turn, carry):
        blk = (2 * turn) % n + (2 * turn) // n
        first_pos = sb[blk] * tok
        span = NPREV + first_pos // span_len
        local_first = first_pos % span_len + s * half
        in_span = sb[blk] % (n // 2)

        def query_set(cosine, sine):
            return jnp.concatenate(
                [rope_rows(qf[blk, g], cosine, sine) for g in range(G)], axis=0
            ).astype(jnp.bfloat16)

        q_intra = query_set(block_rows(rope_c, in_span, 0), block_rows(rope_s, in_span, 0))
        q_succ = query_set(
            block_rows(rope_c, in_span, span_len), block_rows(rope_s, in_span, span_len)
        )
        q_inter = query_set(rope_c[last : last + 1, :], rope_s[last : last + 1, :])
        pieces = []
        for j in range(n):
            key_first = sb[j] * tok
            key_span = NPREV + key_first // span_len
            same = key_span == span
            reach = jnp.where(same, local_first - key_first % span_len, -2 * span_len)
            reach = jnp.where(key_span == span - 1, 2 * span_len, reach)
            query = jnp.where(same, q_intra, q_succ)
            score = scores_of(query, kv[:, 0, j].reshape(tok, HD))
            score = jnp.where(ahead <= reach, score, neg_big)
            pieces.append((score, kv[:, 1, j].reshape(tok, HD)))
        per_span = n // NPREV
        for b in range(NPREV):
            block = old[:, b * per_span : (b + 1) * per_span]
            size = 2 * per_span * half
            query = q_inter
            if b == NPREV - 1:
                query = jnp.where(span - 1 == b, q_succ, q_inter)
            score = scores_of(query, block[:, :, 0].reshape(size, HD))
            pieces.append((score, block[:, :, 1].reshape(size, HD)))
        top = functools.reduce(
            jnp.maximum, [jnp.max(score, axis=1, keepdims=True) for score, _ in pieces]
        )
        weight_sum = jnp.zeros((row_count, 1), jnp.float32)
        weighted = jnp.zeros((row_count, HD), jnp.float32)
        for score, value in pieces:
            weights = jnp.exp2((score - top) * power)
            weight_sum = weight_sum + jnp.sum(weights, axis=1, keepdims=True)
            weighted = weighted + jnp.dot(
                weights.astype(jnp.bfloat16), value, preferred_element_type=jnp.float32
            )
        result = (weighted / weight_sum).astype(jnp.bfloat16)
        for g in range(G):
            ho[turn, :, g * HD : (g + 1) * HD] = result[g * half : (g + 1) * half]

        def keep(j):
            first = (j * rows_out) // LANE * LANE
            a2[j, turn] = ho[turn, :, first : first + a2.shape[3]]

        for j in range(n):
            pl.when(c == j)(functools.partial(keep, j))
        others(lambda j: head_copy(turn, j, c).start())
        return carry

    def heads_ready(turn, carry):
        others(lambda j: head_copy(turn, j, j).wait_recv())
        return carry

    def product(part_index, column_first):
        columns = pl.ds(pl.multiple_of(column_first, LANE), chunk)
        total = None
        for j in range(n):
            rows = a2[j, part_index * per_half : (part_index + 1) * per_half]
            term = jnp.dot(
                rows.reshape(per_half * half, a2.shape[3]), wo[j, :, columns],
                preferred_element_type=jnp.float32,
            )
            total = term if total is None else total + term
        return total.reshape(per_half, half, chunk)

    width = chunk * chunks

    def x_copy(m):
        return remote(xs.at[m], xr.at[m], cs_sem.at[m], cr_sem.at[m], head=oh)

    def z_copy(q, k, i, src_ctx):
        return remote(
            zs.at[q * chunks + k, i], zr.at[src_ctx, k],
            ds_sem.at[q * chunks + k, i], dr_sem.at[src_ctx, k], ctx=2 * i + q,
        )

    def send_half(q):
        def send(k, carry):
            m = q * chunks + k
            xs[m] = product(q, oh * width + k * chunk).astype(jnp.bfloat16)
            x_copy(m).start()
            return carry

        lax.fori_loop(0, chunks, send, 0)

    def own_half(q):
        def compute(k, carry):
            ow[q * chunks + k] = product(q, hx * width + k * chunk)
            return carry

        lax.fori_loop(0, chunks, compute, 0)

    def to_owners(q, action):
        for i in range(per_half):
            pl.when(c != 2 * i + q)(functools.partial(action, i))

    def add_half(q):
        def add(k, carry):
            m = q * chunks + k
            x_copy(m).wait_recv()
            zs[m] = (ow[m] + xr[m].astype(jnp.float32)).astype(jnp.bfloat16)
            to_owners(q, lambda i: z_copy(q, k, i, c).start())

            def keep(i):
                zr[2 * i + q, k] = zs[m, i]

            for i in range(per_half):
                pl.when(c == 2 * i + q)(functools.partial(keep, i))
            return carry

        lax.fori_loop(0, chunks, add, 0)

    lax.fori_loop(0, n - 1, attend, 0)
    load_wo.wait()
    lax.fori_loop(0, per_half, heads_ready, 0)
    send_half(0)
    lax.fori_loop(n - 1, n, attend, 0)
    own_half(0)
    lax.fori_loop(per_half, n, heads_ready, 0)
    send_half(1)
    add_half(0)
    own_half(1)
    add_half(1)

    for k in range(chunks):
        others(lambda j: z_copy(0, k, 0, j).wait_recv())
        total = zr[0, k].astype(jnp.float32)
        for j in range(1, n):
            total = total + zr[j, k].astype(jnp.float32)
        out_ref[:, k * chunk : (k + 1) * chunk] = total.astype(jnp.bfloat16)

    old_pair.wait_send()
    kv_pair.wait_send()
    others(lambda j: old_copy(j, c).wait_send())
    part_copy(c).wait_send()
    for p in range(ROW_PIECES):
        pl.when(c + 1 < n)(lambda: to_right(x_ref, c, p).wait_send())
        pl.when(c > 0)(lambda: to_left(x_ref, c, p).wait_send())

    def sent(distance, carry):
        left = c - distance
        right = c + distance

        def left_sent():
            for p in range(ROW_PIECES):
                pl.when(c + 1 < n)(lambda: to_right(hid.at[left], left, p).wait_send())
                over_x(left, hx, p).wait_send()
            part_copy(left).wait_send()

        def right_sent():
            for p in range(ROW_PIECES):
                pl.when(c > 0)(lambda: to_left(hid.at[right], right, p).wait_send())
                over_x(right, hx, p).wait_send()
            part_copy(right).wait_send()

        pl.when(left >= 0)(left_sent)
        pl.when(right < n)(right_sent)
        return carry

    lax.fori_loop(1, n, sent, 0)

    def block_sent(blk, carry):
        others(lambda j: piece_copy(blk, j, c).wait_send())
        others(lambda j: head_copy(blk, j, c).wait_send())
        return carry

    lax.fori_loop(0, n, block_sent, 0)

    for q in range(2):
        def chunk_sent(k, carry):
            x_copy(q * chunks + k).wait_send()
            to_owners(q, lambda i: z_copy(q, k, i, c).wait_send())
            return carry

        lax.fori_loop(0, chunks, chunk_sent, 0)


def rope_tables(count):
    frequency = np.float32(rope_base) ** (
        -(np.arange(HD // 2, dtype=np.float32) * np.float32(2.0)) / np.float32(HD)
    )
    angles = np.arange(count, dtype=np.float32)[:, None] * frequency.astype(np.float32)[None, :]
    cosine = np.cos(angles.astype(np.float64)).astype(np.float32)
    sine = np.sin(angles.astype(np.float64)).astype(np.float32)
    return (
        np.concatenate([cosine, cosine], axis=1),
        np.concatenate([-sine, sine], axis=1),
    )


def local_fused(hidden_in, w_qkv, qkv_bias, w_out, prev_keys, prev_values, shard_blocks):
    n = lax.axis_size("ctx")
    tok, features = hidden_in.shape
    half = tok // 2
    piece = w_qkv.shape[2]
    wide = round_up(piece, LANE)
    rows_out, model = w_out.shape[1:]
    window = 2 * LANE
    chunks = OUT_CHUNKS
    chunk = model // 2 // chunks
    c = lax.axis_index("ctx")
    bias = lax.dynamic_slice_in_dim(qkv_bias, c * piece, piece, 1).astype(jnp.float32)
    bias = jnp.pad(bias, ((0, 0), (0, wide - piece)))
    earlier = jnp.transpose(jnp.stack([prev_keys, prev_values]), (2, 0, 1, 3))
    cosine, sine = rope_tables(tok * n)
    bf16, f32, dma = jnp.bfloat16, jnp.float32, pltpu.SemaphoreType.DMA
    vmem = pl.BlockSpec(memory_space=pltpu.VMEM)
    smem = pl.BlockSpec(memory_space=pltpu.SMEM)
    hbm = pl.BlockSpec(memory_space=pl.ANY)
    return pl.pallas_call(
        fused,
        out_shape=jax.ShapeDtypeStruct((half, model // 2), bf16),
        in_specs=[smem, vmem, vmem, vmem, vmem, vmem, hbm, hbm],
        out_specs=vmem,
        scratch_shapes=[
            pltpu.VMEM((n, tok, features), bf16),
            pltpu.VMEM((n, wide, features), bf16),
            pltpu.VMEM((n, window, model), bf16),
            pltpu.VMEM((n, 2, n, half, wide), f32),
            pltpu.VMEM((n, n, half, wide), f32),
            pltpu.VMEM((n, n, half, wide), bf16),
            pltpu.VMEM((n, n, half, wide), bf16),
            pltpu.VMEM((2, 2, n, half, HD), bf16),
            pltpu.VMEM((2, n, 2, half, HD), bf16),
            pltpu.VMEM((n, G, half, HD), f32),
            pltpu.VMEM((n, half, G * HD), bf16),
            pltpu.VMEM((n, n, half, window), bf16),
            pltpu.VMEM((2 * chunks, n // 2, half, chunk), bf16),
            pltpu.VMEM((2 * chunks, n // 2, half, chunk), bf16),
            pltpu.VMEM((2 * chunks, n // 2, half, chunk), f32),
            pltpu.VMEM((2 * chunks, n // 2, half, chunk), bf16),
            pltpu.VMEM((n, chunks, half, chunk), bf16),
            dma((2,)), *[dma((n, ROW_PIECES))] * 5, dma((n,)), dma((n,)),
            dma((n, n)), dma((n, n)), dma((n,)), dma((n,)), dma((4,)), dma((n, n)), dma((n, n)),
            dma((2 * chunks,)), dma((2 * chunks,)), dma((2 * chunks, n // 2)), dma((n, chunks)),
        ],
        compiler_params=pltpu.CompilerParams(
            collective_id=0, has_side_effects=True, vmem_limit_bytes=56 * 2**20
        ),
    )(
        shard_blocks, hidden_in, earlier, bias, jnp.asarray(cosine), jnp.asarray(sine),
        jnp.transpose(w_qkv, (1, 2, 0)), w_out,
    )


def choose(hidden_in, w_qkv, qkv_bias, w_out, prev_keys, prev_values, shard_blocks):
    n = lax.axis_size("ctx")
    tok = hidden_in.shape[0]
    rows_out, model = w_out.shape[1:]
    offsets = [(j * rows_out) % LANE for j in range(n)]
    fits = (
        lax.axis_size("sub") == 2
        and lax.axis_size("head") == 2
        and w_qkv.shape[1] == n
        and n % NPREV == 0
        and n > 2
        and tok % (32 * ROW_PIECES) == 0
        and w_qkv.shape[2] % 16 == 0
        and rows_out % 16 == 0
        and max(offsets) + rows_out <= 2 * LANE
        and ((n - 1) * rows_out) // LANE * LANE + 2 * LANE <= G * HD
        and model % (2 * OUT_CHUNKS * LANE) == 0
    )
    body = local_fused if fits else local
    return body(hidden_in, w_qkv, qkv_bias, w_out, prev_keys, prev_values, shard_blocks)


def solution(mesh):
    return jax.shard_map(
        choose,
        mesh=mesh,
        in_specs=(
            P(("groups", "ctx"), "sub"),
            P("sub", "head", "ctx"),
            P("head", None),
            P("head", "ctx", None),
            P(("groups", "ctx", "sub"), "head", None),
            P(("groups", "ctx", "sub"), "head", None),
            P("groups"),
        ),
        out_specs=P(("groups", "ctx", "sub"), "head"),
        check_vma=False,
    )
```

```python
import functools
import math

import jax
import jax.numpy as jnp
import numpy as np
from jax import lax
from jax.experimental import pallas as pl
from jax.experimental.pallas import tpu as pltpu
from jax.sharding import PartitionSpec as P

G = 5
HD = 128
NPREV = 2


rope_base = 10000000.0
neg_big = -1e30


def rotate(vectors, positions):
    half_width = vectors.shape[-1] // 2
    frequency = rope_base ** (
        -(jnp.arange(half_width, dtype=jnp.float32) * 2.0) / vectors.shape[-1]
    )
    angles = positions.astype(jnp.float32)[:, None] * frequency[None, :]
    extra = (1,) * (vectors.ndim - 2)
    cosine = jnp.cos(angles).reshape((angles.shape[0],) + extra + (half_width,))
    sine_part = jnp.sin(angles).reshape((angles.shape[0],) + extra + (half_width,))
    first = vectors[..., :half_width]
    second = vectors[..., half_width:]
    return jnp.concatenate(
        [first * cosine - second * sine_part, second * cosine + first * sine_part], axis=-1
    )


def lookup(small_table, wanted):
    entries = jnp.arange(small_table.shape[0], dtype=jnp.int32)
    return jnp.sum(jnp.where(wanted[..., None] == entries, small_table, 0), axis=-1)


def local(hidden_in, w_qkv, qkv_bias, w_out, prev_keys, prev_values, shard_blocks):
    n_ctx = lax.axis_size("ctx")
    n_sub = lax.axis_size("sub")
    n_head = lax.axis_size("head")
    tok_ctx = hidden_in.shape[0]
    tok_dev = tok_ctx // n_sub
    span_len = tok_ctx * n_ctx // 2
    kv_dev = w_qkv.shape[1]
    me_ctx = lax.axis_index("ctx")
    me_sub = lax.axis_index("sub")
    partial_value = jnp.einsum(
        "td,dhn->thn",
        hidden_in,
        lax.all_gather(w_qkv, "ctx", axis=2, tiled=True),
        preferred_element_type=jnp.float32,
    )
    joined = lax.psum_scatter(partial_value, "sub", scatter_dimension=0, tiled=True)
    joined = (joined + qkv_bias.astype(jnp.float32)[None]).reshape(tok_dev, kv_dev, G + 2, HD)
    owner_block = lookup(shard_blocks, me_ctx)
    positions = owner_block * tok_ctx + me_sub * tok_dev + jnp.arange(tok_dev, dtype=jnp.int32)
    span_q = NPREV + positions // span_len
    local_q = positions % span_len
    queries = joined[:, :, :G]

    def arrange(rotated):
        return jnp.transpose(rotated.astype(jnp.bfloat16), (1, 0, 2, 3)).reshape(
            kv_dev, tok_dev * G, HD
        )

    q_intra = arrange(rotate(queries, local_q))
    q_succ = arrange(rotate(queries, local_q + span_len))
    q_inter = arrange(rotate(queries, jnp.full((tok_dev,), 2 * span_len - 1, jnp.int32)))
    k_cur = rotate(joined[:, :, G], local_q).astype(jnp.bfloat16)
    v_cur = joined[:, :, G + 1].astype(jnp.bfloat16)
    old_rows = (me_ctx * n_sub + me_sub) * tok_dev + jnp.arange(tok_dev, dtype=jnp.int32)
    k_prev = rotate(prev_keys.astype(jnp.float32), old_rows % span_len).astype(jnp.bfloat16)
    row_span = jnp.repeat(span_q, G)
    row_local = jnp.repeat(local_q, G)
    own_span = span_q[0]
    score_scale = HD ** (-0.5)
    row_count = tok_dev * G
    start_state = (
        jnp.full((kv_dev, row_count), neg_big, jnp.float32),
        jnp.zeros((kv_dev, row_count), jnp.float32),
        jnp.zeros((kv_dev, row_count, HD), jnp.float32),
    )

    def scores_of(query_set, key_block):
        return (
            jnp.einsum("hrd,khd->hrk", query_set, key_block, preferred_element_type=jnp.float32)
            * score_scale
        )

    def update(running, scores, allowed, value_block):
        running_max, weight_sum, weighted = running
        block_max = jnp.max(jnp.where(allowed, scores, neg_big), axis=2)
        new_max = jnp.maximum(running_max, block_max)
        weights = jnp.where(allowed, jnp.exp(scores - new_max[..., None]), 0.0)
        rescale = jnp.exp(running_max - new_max)
        weight_sum = weight_sum * rescale + jnp.sum(weights, axis=2)
        weighted = weighted * rescale[..., None] + jnp.einsum(
            "hrk,khd->hrd",
            weights.astype(jnp.bfloat16),
            value_block,
            preferred_element_type=jnp.float32,
        )
        return (new_max, weight_sum, weighted)

    def current_block(running, key_block, value_block, key_index):
        shard_index = key_index // tok_dev
        key_pos = (
            lookup(shard_blocks, shard_index // n_sub) * tok_ctx
            + shard_index % n_sub * tok_dev
            + key_index % tok_dev
        )
        key_span = NPREV + key_pos // span_len
        key_local = key_pos % span_len
        same_span = key_span[None, :] == row_span[:, None]
        before = key_span[None, :] == row_span[:, None] - 1
        allowed = same_span & (key_local[None, :] <= row_local[:, None]) | before
        query_set = jnp.where(key_span[0] == own_span, q_intra, q_succ)
        return update(running, scores_of(query_set, key_block), allowed[None], value_block)

    def earlier_block(running, key_block, value_block, key_index):
        block_span = key_index[0] // span_len
        query_set = jnp.where(block_span == own_span - 1, q_succ, q_inter)
        scores = scores_of(query_set, key_block)
        return update(running, scores, jnp.ones(scores.shape, jnp.bool_), value_block)

    cur_keys = lax.all_gather(k_cur, ("ctx", "sub"), axis=0, tiled=True)
    cur_values = lax.all_gather(v_cur, ("ctx", "sub"), axis=0, tiled=True)
    old_keys = lax.all_gather(k_prev, ("ctx", "sub"), axis=0, tiled=True)
    old_values = lax.all_gather(prev_values, ("ctx", "sub"), axis=0, tiled=True)
    piece_rows = cur_keys.shape[0]
    block_rows = math.gcd(piece_rows, tok_dev)

    def turn(turn_index, state_in):
        offset = turn_index * block_rows
        key_index = offset + jnp.arange(block_rows, dtype=jnp.int32)

        def take(values):
            return lax.dynamic_slice_in_dim(values, offset, block_rows, 0)

        state_in = current_block(state_in, take(cur_keys), take(cur_values), key_index)
        return earlier_block(state_in, take(old_keys), take(old_values), key_index)

    running_max, weight_sum, weighted = lax.fori_loop(
        0, piece_rows // block_rows, turn, start_state
    )
    head_out = (weighted / weight_sum[..., None]).astype(jnp.bfloat16)
    head_out = jnp.transpose(head_out.reshape(kv_dev, tok_dev, G, HD), (1, 0, 2, 3)).reshape(
        tok_dev, kv_dev, G * HD
    )
    group_cols = w_out.shape[2] // (n_head * n_sub)
    split_cols = w_out.reshape(kv_dev, w_out.shape[1], n_head, n_sub, group_cols)
    own_cols = lax.dynamic_index_in_dim(split_cols, me_sub, 3, keepdims=False).reshape(
        kv_dev, w_out.shape[1], n_head * group_cols
    )
    pair_heads = lax.all_gather(head_out, "sub", axis=0, tiled=True)
    summed = jnp.einsum(
        "thn,hnd->td",
        pair_heads,
        lax.all_gather(own_cols, "ctx", axis=1, tiled=True),
        preferred_element_type=jnp.float32,
    )
    shares = lax.psum_scatter(summed.astype(jnp.bfloat16), "head", scatter_dimension=1, tiled=True)
    return lax.all_to_all(shares, "sub", split_axis=0, concat_axis=1, tiled=True)


MESH = pl.DeviceIdType.MESH
LANE = 128
OUT_CHUNKS = 5
ROW_PIECES = 2


def round_up(value, step):
    return (value + step - 1) // step * step


def remote(src, dst, send_sem, recv_sem, **where):
    return pltpu.make_async_remote_copy(
        src_ref=src, dst_ref=dst, send_sem=send_sem, recv_sem=recv_sem,
        device_id=where, device_id_type=MESH,
    )


def rope_rows(vectors, cosine, sine):
    return vectors * cosine + pltpu.roll(vectors, HD // 2, 1) * sine


def fused(
    sb, x_ref, pv_ref, bias, rope_c, rope_s, w_hbm, wo_hbm, out_ref,
    hid, wv, wo, part, prcv, jb, ar, kv, old, qf, ho, a2, a2r, xs, xr, ow, zs, zr,
    w_sem, zsr_sem, zsl_sem, zrv_sem, hs_sem, hr_sem, ps_sem, pr_sem, as_sem, ar_sem,
    os_sem, or_sem, ex_sem, bs_sem, br_sem, cs_sem, cr_sem, ds_sem, dr_sem,
):
    n = hid.shape[0]
    tok = hid.shape[1]
    half = tok // 2
    span_len = tok * n // 2
    piece = w_hbm.shape[1]
    wide = wv.shape[1]
    rows_out = wo_hbm.shape[1]
    per_half = xs.shape[1]
    chunk = xs.shape[3]
    chunks = zr.shape[1]
    c = lax.axis_index("ctx")
    hx = lax.axis_index("head")
    s = lax.axis_index("sub")
    oh = 1 - hx
    other = 1 - s

    def others(action):
        for j in range(n):
            pl.when(c != j)(functools.partial(action, j))

    for h in range(n):
        wv[h, piece:, :] = jnp.zeros((wide - piece, wv.shape[2]), jnp.bfloat16)
    load_w = pltpu.make_async_copy(w_hbm, wv.at[:, pl.ds(0, piece), :], w_sem.at[0])
    load_w.start()

    barrier = pltpu.get_barrier_semaphore()

    def greet(j):
        pl.semaphore_signal(barrier, inc=1, device_id={"ctx": j}, device_id_type=MESH)

    others(greet)
    pl.semaphore_signal(barrier, inc=1, device_id={"head": oh}, device_id_type=MESH)
    pl.semaphore_signal(barrier, inc=1, device_id={"sub": other}, device_id_type=MESH)
    pl.semaphore_wait(barrier, n + 1)

    sliver = half // ROW_PIECES

    def rows_of(chip, p):
        return pl.ds(pl.multiple_of(chip * half + p * sliver, sliver), sliver)

    def to_right(src, blk, p):
        rows = rows_of(hx, p)
        return remote(
            src.at[rows], hid.at[blk, rows], zsr_sem.at[blk, p], zrv_sem.at[blk, p], ctx=c + 1
        )

    def to_left(src, blk, p):
        rows = rows_of(hx, p)
        return remote(
            src.at[rows], hid.at[blk, rows], zsl_sem.at[blk, p], zrv_sem.at[blk, p], ctx=c - 1
        )

    def over_x(blk, chip, p):
        rows = rows_of(chip, p)
        return remote(
            hid.at[blk, rows], hid.at[blk, rows], hs_sem.at[blk, p], hr_sem.at[blk, p], head=oh
        )

    for p in range(ROW_PIECES):
        pl.when(c + 1 < n)(lambda: to_right(x_ref, c, p).start())
        pl.when(c > 0)(lambda: to_left(x_ref, c, p).start())

    def old_copy(j, src_ctx):
        return remote(pv_ref.at[j], old.at[s, src_ctx], os_sem.at[j], or_sem.at[src_ctx], ctx=j)

    others(lambda j: old_copy(j, c).start())
    old[s, c] = pv_ref[c]

    wo[...] = jnp.zeros(wo.shape, jnp.bfloat16)
    rest = rows_out - LANE
    groups = LANE // rest

    def load_rows(u):
        target = LANE if u == groups else pl.multiple_of(((u + c) % groups) * rest, rest)
        return pltpu.make_async_copy(
            wo_hbm.at[:, pl.ds(u * rest, rest), :], wo.at[:, pl.ds(target, rest), :],
            w_sem.at[1 + u],
        )

    for u in range(groups + 1):
        load_rows(u).start()
    load_w.wait()

    def part_copy(blk):
        return remote(part.at[blk, other], prcv.at[blk], ps_sem.at[blk], pr_sem.at[blk], sub=other)

    def piece_copy(blk, j, src_ctx):
        return remote(
            jb.at[blk, j], ar.at[src_ctx, blk], as_sem.at[blk, j], ar_sem.at[src_ctx, blk], ctx=j
        )

    def project(blk, rows):
        for h in range(n):
            product = lax.dot_general(
                rows, wv[h], (((1,), (1,)), ((), ())), preferred_element_type=jnp.float32
            )
            part[blk, 0, h] = product[:half]
            part[blk, 1, h] = product[half:]
        part_copy(blk).start()

    def finish(blk):
        part_copy(blk).wait_recv()
        for h in range(n):
            joined = part[blk, s, h] + prcv[blk, h] + bias[h : h + 1, :]
            jb[blk, h] = joined.astype(jnp.bfloat16)
        ar[c, blk] = jb[blk, c]
        others(lambda j: piece_copy(blk, j, c).start())

    def pass_on(distance, p):
        left = c - distance
        right = c + distance

        def from_left():
            to_right(hid.at[left], left, p).wait_recv()
            pl.when(c + 1 < n)(lambda: to_right(hid.at[left], left, p).start())
            over_x(left, hx, p).start()

        def from_right():
            to_left(hid.at[right], right, p).wait_recv()
            pl.when(c > 0)(lambda: to_left(hid.at[right], right, p).start())
            over_x(right, hx, p).start()

        pl.when(left >= 0)(from_left)
        pl.when(right < n)(from_right)

    def use(blk):
        for p in range(ROW_PIECES):
            over_x(blk, oh, p).wait_recv()
        project(blk, hid[blk])

    def both(distance, action, p=None):
        left = c - distance
        right = c + distance
        if p != 1:
            pl.when(left >= 0)(lambda: action(left))
        if p != 0:
            pl.when(right < n)(lambda: action(right))

    def arrive(distance, carry):
        pass_on(distance, 0)
        both(distance - 1, use, 0)
        pass_on(distance, 1)
        both(distance - 1, use, 1)
        pl.when(distance == 2)(lambda: finish(c))
        pl.when(distance > 2)(lambda: both(distance - 2, finish))
        return carry

    pass_on(1, 0)
    project(c, x_ref[...])
    pass_on(1, 1)
    lax.fori_loop(2, n, arrive, 0)
    both(n - 2, finish)
    both(n - 1, use)
    both(n - 1, finish)

    def old_ready(j):
        old_copy(j, j).wait_recv()

    others(old_ready)
    for j in range(n):
        at = pl.ds(pl.multiple_of(((j * 2 + s) * half) % span_len, half), half)
        raw = old[s, j, 0].astype(jnp.float32)
        old[s, j, 0] = rope_rows(raw, rope_c[at, :], rope_s[at, :]).astype(jnp.bfloat16)
    old_pair = remote(old.at[s], old.at[s], ex_sem.at[0], ex_sem.at[1], sub=other)
    old_pair.start()

    lane = lax.broadcasted_iota(jnp.int32, (half, LANE), 1)

    def block_rows(table, in_span, first):
        chosen = None
        for v in range(n // 2):
            rows = table[pl.ds(pl.multiple_of(first + v * tok + s * half, half), half), :]
            chosen = rows if chosen is None else jnp.where(in_span == v, rows, chosen)
        return chosen

    def gather_head(blk, carry):
        others(lambda j: piece_copy(blk, j, j).wait_recv())
        got = [ar[j, blk].astype(jnp.float32) for j in range(n)]
        columns = []
        for b in range(G + 2):
            total = None
            for j in range(n):
                shift = b * LANE - j * piece
                if shift <= -LANE or shift >= piece:
                    continue
                moved = pltpu.roll(got[j], (-shift) % wide, 1)[:, :LANE]
                inside = (lane + shift >= 0) & (lane + shift < piece)
                moved = jnp.where(inside, moved, 0.0)
                total = moved if total is None else total + moved
            columns.append(total)
        for g in range(G):
            qf[blk, g] = columns[g]
        in_span = sb[blk] % (n // 2)
        cosine, sine = block_rows(rope_c, in_span, 0), block_rows(rope_s, in_span, 0)
        kv[s, 0, blk] = rope_rows(columns[G], cosine, sine).astype(jnp.bfloat16)
        kv[s, 1, blk] = columns[G + 1].astype(jnp.bfloat16)
        return carry

    lax.fori_loop(0, n, gather_head, 0)
    kv_pair = remote(kv.at[s], kv.at[s], ex_sem.at[2], ex_sem.at[3], sub=other)
    kv_pair.start()
    remote(old.at[other], old.at[other], ex_sem.at[0], ex_sem.at[1], sub=other).wait_recv()
    remote(kv.at[other], kv.at[other], ex_sem.at[2], ex_sem.at[3], sub=other).wait_recv()

    row_count = half * G
    key = lax.broadcasted_iota(jnp.int32, (row_count, tok), 1)
    row = lax.broadcasted_iota(jnp.int32, (row_count, tok), 0) % half
    ahead = key - row
    last = 2 * span_len - 1
    power = HD ** (-0.5) * math.log2(math.e)

    def scores_of(query, keys):
        return lax.dot_general(
            query, keys, (((1,), (1,)), ((), ())), preferred_element_type=jnp.float32
        )

    def head_copy(blk, j, src_ctx):
        return remote(
            ho.at[blk, j], a2r.at[src_ctx, blk],
            bs_sem.at[blk, j], br_sem.at[src_ctx, blk], ctx=j,
        )

    def attend(turn, carry):
        blk = (2 * turn) % n + (2 * turn) // n
        first_pos = sb[blk] * tok
        span = NPREV + first_pos // span_len
        local_first = first_pos % span_len + s * half
        in_span = sb[blk] % (n // 2)

        def query_set(cosine, sine):
            return jnp.concatenate(
                [rope_rows(qf[blk, g], cosine, sine) for g in range(G)], axis=0
            ).astype(jnp.bfloat16)

        q_intra = query_set(block_rows(rope_c, in_span, 0), block_rows(rope_s, in_span, 0))
        q_succ = query_set(
            block_rows(rope_c, in_span, span_len), block_rows(rope_s, in_span, span_len)
        )
        q_inter = query_set(rope_c[last : last + 1, :], rope_s[last : last + 1, :])
        pieces = []
        for j in range(n):
            key_first = sb[j] * tok
            key_span = NPREV + key_first // span_len
            same = key_span == span
            reach = jnp.where(same, local_first - key_first % span_len, -2 * span_len)
            reach = jnp.where(key_span == span - 1, 2 * span_len, reach)
            query = jnp.where(same, q_intra, q_succ)
            score = scores_of(query, kv[:, 0, j].reshape(tok, HD))
            score = jnp.where(ahead <= reach, score, neg_big)
            pieces.append((score, kv[:, 1, j].reshape(tok, HD)))
        per_span = n // NPREV
        for b in range(NPREV):
            block = old[:, b * per_span : (b + 1) * per_span]
            size = 2 * per_span * half
            query = q_inter
            if b == NPREV - 1:
                query = jnp.where(span - 1 == b, q_succ, q_inter)
            score = scores_of(query, block[:, :, 0].reshape(size, HD))
            pieces.append((score, block[:, :, 1].reshape(size, HD)))
        top = functools.reduce(
            jnp.maximum, [jnp.max(score, axis=1, keepdims=True) for score, _ in pieces]
        )
        weight_sum = jnp.zeros((row_count, 1), jnp.float32)
        weighted = jnp.zeros((row_count, HD), jnp.float32)
        for score, value in pieces:
            weights = jnp.exp2((score - top) * power)
            weight_sum = weight_sum + jnp.sum(weights, axis=1, keepdims=True)
            weighted = weighted + jnp.dot(
                weights.astype(jnp.bfloat16), value, preferred_element_type=jnp.float32
            )
        result = (weighted / weight_sum).astype(jnp.bfloat16).astype(jnp.float32)
        few = half // groups
        few_lane = lane[:few]
        for j in range(n):
            first = result[j * half : (j + 1) * half]
            second = result[(j + 1) * half : (j + 2) * half]
            full = jnp.where(lane >= j * rest, first, second)
            packed = jnp.zeros((few, LANE), jnp.float32)
            for u in range(groups):
                rows = second[u * few : (u + 1) * few]
                shift = ((u - j) * rest) % LANE
                moved = pltpu.roll(rows, shift, 1) if shift else rows
                inside = (few_lane >= u * rest) & (few_lane < (u + 1) * rest)
                packed = packed + jnp.where(inside, moved, 0.0)
            ho[turn, j, :half, :] = full.astype(jnp.bfloat16)
            ho[turn, j, half:, :] = packed.astype(jnp.bfloat16)

        a2r[c, turn] = ho[turn, c]
        others(lambda j: head_copy(turn, j, c).start())
        return carry

    def heads_ready(turn, carry):
        others(lambda j: head_copy(turn, j, j).wait_recv())
        few = half // groups
        for j in range(n):
            a2[j, turn, :, :LANE] = a2r[j, turn, :half, :]
            packed = a2r[j, turn, half:, :].astype(jnp.float32)
            for u in range(groups):
                moved = pltpu.roll(packed, (LANE - u * rest) % LANE, 1) if u else packed
                a2[j, turn, u * few : (u + 1) * few, LANE:] = moved.astype(jnp.bfloat16)
        return carry

    def product(part_index, column_first):
        columns = pl.ds(pl.multiple_of(column_first, LANE), chunk)
        total = None
        for j in range(n):
            rows = a2[j, part_index * per_half : (part_index + 1) * per_half]
            term = jnp.dot(
                rows.reshape(per_half * half, a2.shape[3]), wo[j, :, columns],
                preferred_element_type=jnp.float32,
            )
            total = term if total is None else total + term
        return total.reshape(per_half, half, chunk)

    width = chunk * chunks

    def x_copy(m):
        return remote(xs.at[m], xr.at[m], cs_sem.at[m], cr_sem.at[m], head=oh)

    def z_copy(q, k, i, src_ctx):
        return remote(
            zs.at[q * chunks + k, i], zr.at[src_ctx, k],
            ds_sem.at[q * chunks + k, i], dr_sem.at[src_ctx, k], ctx=2 * i + q,
        )

    def send_half(q):
        def send(k, carry):
            m = q * chunks + k
            xs[m] = product(q, oh * width + k * chunk).astype(jnp.bfloat16)
            x_copy(m).start()
            return carry

        lax.fori_loop(0, chunks, send, 0)

    def own_half(q):
        def compute(k, carry):
            ow[q * chunks + k] = product(q, hx * width + k * chunk)
            return carry

        lax.fori_loop(0, chunks, compute, 0)

    def to_owners(q, action):
        for i in range(per_half):
            pl.when(c != 2 * i + q)(functools.partial(action, i))

    def add_half(q):
        def add(k, carry):
            m = q * chunks + k
            x_copy(m).wait_recv()
            zs[m] = (ow[m] + xr[m].astype(jnp.float32)).astype(jnp.bfloat16)
            to_owners(q, lambda i: z_copy(q, k, i, c).start())

            def keep(i):
                zr[2 * i + q, k] = zs[m, i]

            for i in range(per_half):
                pl.when(c == 2 * i + q)(functools.partial(keep, i))
            return carry

        lax.fori_loop(0, chunks, add, 0)

    lax.fori_loop(0, n - 1, attend, 0)
    for u in range(groups + 1):
        load_rows(u).wait()
    lax.fori_loop(0, per_half, heads_ready, 0)
    send_half(0)
    lax.fori_loop(n - 1, n, attend, 0)
    own_half(0)
    lax.fori_loop(per_half, n, heads_ready, 0)
    send_half(1)
    add_half(0)
    own_half(1)
    add_half(1)

    for k in range(chunks):
        others(lambda j: z_copy(0, k, 0, j).wait_recv())
        total = zr[0, k].astype(jnp.float32)
        for j in range(1, n):
            total = total + zr[j, k].astype(jnp.float32)
        out_ref[:, k * chunk : (k + 1) * chunk] = total.astype(jnp.bfloat16)

    old_pair.wait_send()
    kv_pair.wait_send()
    others(lambda j: old_copy(j, c).wait_send())
    part_copy(c).wait_send()
    for p in range(ROW_PIECES):
        pl.when(c + 1 < n)(lambda: to_right(x_ref, c, p).wait_send())
        pl.when(c > 0)(lambda: to_left(x_ref, c, p).wait_send())

    def sent(distance, carry):
        left = c - distance
        right = c + distance

        def left_sent():
            for p in range(ROW_PIECES):
                pl.when(c + 1 < n)(lambda: to_right(hid.at[left], left, p).wait_send())
                over_x(left, hx, p).wait_send()
            part_copy(left).wait_send()

        def right_sent():
            for p in range(ROW_PIECES):
                pl.when(c > 0)(lambda: to_left(hid.at[right], right, p).wait_send())
                over_x(right, hx, p).wait_send()
            part_copy(right).wait_send()

        pl.when(left >= 0)(left_sent)
        pl.when(right < n)(right_sent)
        return carry

    lax.fori_loop(1, n, sent, 0)

    def block_sent(blk, carry):
        others(lambda j: piece_copy(blk, j, c).wait_send())
        others(lambda j: head_copy(blk, j, c).wait_send())
        return carry

    lax.fori_loop(0, n, block_sent, 0)

    for q in range(2):
        def chunk_sent(k, carry):
            x_copy(q * chunks + k).wait_send()
            to_owners(q, lambda i: z_copy(q, k, i, c).wait_send())
            return carry

        lax.fori_loop(0, chunks, chunk_sent, 0)


def rope_tables(count):
    frequency = np.float32(rope_base) ** (
        -(np.arange(HD // 2, dtype=np.float32) * np.float32(2.0)) / np.float32(HD)
    )
    angles = np.arange(count, dtype=np.float32)[:, None] * frequency.astype(np.float32)[None, :]
    cosine = np.cos(angles.astype(np.float64)).astype(np.float32)
    sine = np.sin(angles.astype(np.float64)).astype(np.float32)
    return (
        np.concatenate([cosine, cosine], axis=1),
        np.concatenate([-sine, sine], axis=1),
    )


def local_fused(hidden_in, w_qkv, qkv_bias, w_out, prev_keys, prev_values, shard_blocks):
    n = lax.axis_size("ctx")
    tok, features = hidden_in.shape
    half = tok // 2
    piece = w_qkv.shape[2]
    wide = round_up(piece, LANE)
    rows_out, model = w_out.shape[1:]
    window = 2 * LANE
    groups = LANE // (rows_out - LANE)
    send_rows = half + half // groups
    chunks = OUT_CHUNKS
    chunk = model // 2 // chunks
    c = lax.axis_index("ctx")
    bias = lax.dynamic_slice_in_dim(qkv_bias, c * piece, piece, 1).astype(jnp.float32)
    bias = jnp.pad(bias, ((0, 0), (0, wide - piece)))
    earlier = jnp.transpose(jnp.stack([prev_keys, prev_values]), (2, 0, 1, 3))
    cosine, sine = rope_tables(tok * n)
    bf16, f32, dma = jnp.bfloat16, jnp.float32, pltpu.SemaphoreType.DMA
    vmem = pl.BlockSpec(memory_space=pltpu.VMEM)
    smem = pl.BlockSpec(memory_space=pltpu.SMEM)
    hbm = pl.BlockSpec(memory_space=pl.ANY)
    return pl.pallas_call(
        fused,
        out_shape=jax.ShapeDtypeStruct((half, model // 2), bf16),
        in_specs=[smem, vmem, vmem, vmem, vmem, vmem, hbm, hbm],
        out_specs=vmem,
        scratch_shapes=[
            pltpu.VMEM((n, tok, features), bf16),
            pltpu.VMEM((n, wide, features), bf16),
            pltpu.VMEM((n, window, model), bf16),
            pltpu.VMEM((n, 2, n, half, wide), f32),
            pltpu.VMEM((n, n, half, wide), f32),
            pltpu.VMEM((n, n, half, wide), bf16),
            pltpu.VMEM((n, n, half, wide), bf16),
            pltpu.VMEM((2, 2, n, half, HD), bf16),
            pltpu.VMEM((2, n, 2, half, HD), bf16),
            pltpu.VMEM((n, G, half, HD), f32),
            pltpu.VMEM((n, n, send_rows, LANE), bf16),
            pltpu.VMEM((n, n, half, window), bf16),
            pltpu.VMEM((n, n, send_rows, LANE), bf16),
            pltpu.VMEM((2 * chunks, n // 2, half, chunk), bf16),
            pltpu.VMEM((2 * chunks, n // 2, half, chunk), bf16),
            pltpu.VMEM((2 * chunks, n // 2, half, chunk), f32),
            pltpu.VMEM((2 * chunks, n // 2, half, chunk), bf16),
            pltpu.VMEM((n, chunks, half, chunk), bf16),
            dma((groups + 2,)), *[dma((n, ROW_PIECES))] * 5, dma((n,)), dma((n,)),
            dma((n, n)), dma((n, n)), dma((n,)), dma((n,)), dma((4,)), dma((n, n)), dma((n, n)),
            dma((2 * chunks,)), dma((2 * chunks,)), dma((2 * chunks, n // 2)), dma((n, chunks)),
        ],
        compiler_params=pltpu.CompilerParams(
            collective_id=0, has_side_effects=True, vmem_limit_bytes=56 * 2**20
        ),
    )(
        shard_blocks, hidden_in, earlier, bias, jnp.asarray(cosine), jnp.asarray(sine),
        jnp.transpose(w_qkv, (1, 2, 0)), w_out,
    )


def choose(hidden_in, w_qkv, qkv_bias, w_out, prev_keys, prev_values, shard_blocks):
    n = lax.axis_size("ctx")
    tok = hidden_in.shape[0]
    rows_out, model = w_out.shape[1:]
    rest = rows_out - LANE
    fits = (
        lax.axis_size("sub") == 2
        and lax.axis_size("head") == 2
        and w_qkv.shape[1] == n
        and n % NPREV == 0
        and n > 2
        and tok % (32 * ROW_PIECES) == 0
        and w_qkv.shape[2] % 16 == 0
        and rows_out % 16 == 0
        and rest > 0
        and LANE == HD
        and n * rest == LANE
        and n + 1 == G
        and tok // 2 * rest % (16 * LANE) == 0
        and model % (2 * OUT_CHUNKS * LANE) == 0
    )
    body = local_fused if fits else local
    return body(hidden_in, w_qkv, qkv_bias, w_out, prev_keys, prev_values, shard_blocks)


def solution(mesh):
    return jax.shard_map(
        choose,
        mesh=mesh,
        in_specs=(
            P(("groups", "ctx"), "sub"),
            P("sub", "head", "ctx"),
            P("head", None),
            P("head", "ctx", None),
            P(("groups", "ctx", "sub"), "head", None),
            P(("groups", "ctx", "sub"), "head", None),
            P("groups"),
        ),
        out_specs=P(("groups", "ctx", "sub"), "head"),
        check_vma=False,
    )
```
